128 devices in a mesh: dp: 4 (over y_hi, core), mp: 32 (over y_lo, x, z).
Axes of the slice: x: 4, y: 4 (y_hi: 2, y_lo: 2; y = y_hi * 2 + y_lo), z: 4, core: 2. Of those that a mesh axis runs over, the one named last changes fastest.
Arguments:
- tokens: bfloat16 [2048, 6144], P(('dp', 'mp')), may hold values from -6 to 6
- norm_gain: float32 [6144], replicated, may hold values from 0.1 to 1.9
- qkv_weight: bfloat16 [6144, 3, 4096], P(None, None, 'mp'), may hold values from -0.078125 to 0.078125
- up_weight: bfloat16 [6144, 12288], P(None, 'mp'), may hold values from -0.078125 to 0.078125
- proj_weight: bfloat16 [4096, 6144], P('mp'), may hold values from -0.09375 to 0.09375
- down_weight: bfloat16 [12288, 6144], P('mp'), may hold values from -0.0546875 to 0.0546875
- query_gain: float32 [128], replicated, may hold values from 0.1 to 1.9
- key_gain: float32 [128], replicated, may hold values from 0.1 to 1.9
- out_grad: bfloat16 [2048, 6144], P(('dp', 'mp')), may hold values from -6 to 6
Outputs:
- token_grad: bfloat16 [2048, 6144], P(('dp', 'mp'))
- norm_gain_grad: float32 [6144], replicated
- qk_gain_grad: float32 [2, 128], replicated
- qkv_grad: float32 [6144, 3, 4096], P('dp', None, 'mp')
- up_grad: float32 [6144, 12288], P('dp', 'mp')
- proj_grad: float32 [4096, 6144], P('mp', 'dp')
- down_grad: float32 [12288, 6144], P('mp', 'dp')
The draws below stay inside these ranges and needn't reach their ends.
All inputs are finite; a program needn't handle non-finite values.
Results may differ from the reference program's by a relative error of at most 0.033.
Values may be sent and summed in bfloat16 or wider, within the bound.
A program may use at most 192 MiB of HBM per device.

```python
import jax
import jax.numpy as jnp
from jax import lax

D = 6144
FF = 12288
HEADS = 32
HEAD_DIM = 128
PATCHES = 256
IMG_DEV = 2
TOKENS = 2048


def block_scale(key, extent, cuts, smallest, top_value):
    factor_of = 1.0
    for dim, shards_of in cuts:
        heights = jax.random.uniform(jax.random.fold_in(jax.random.fold_in(key, 6), dim), (shards_of,), jnp.float32, smallest / len(cuts), top_value / len(cuts))
        factor_of = factor_of * jnp.repeat(jnp.exp(heights), extent[dim] // shards_of).reshape((-1,) + (1,) * (len(extent) - 1 - dim))
    return factor_of


def bell_draw(own_key, shape, deviation, bound, split=(), dtype=jnp.bfloat16):
    result = deviation * jax.random.normal(own_key, shape, jnp.float32)
    if split:
        result = result * block_scale(own_key, shape, split, -0.22, 0.18)
    return jnp.clip(result, -bound, bound).astype(dtype)


def setup_inputs(seed: int = 0) -> dict:
    splits = jax.random.split(jax.random.key(seed), 10)
    tokens = bell_draw(splits[0], (TOKENS, D), 1.0, 6.0, ((0, 128),))
    norm_gain = jnp.clip(1.0 + 0.18 * jax.random.normal(splits[1], (D,), jnp.float32), 0.1, 1.9)
    qkv_weight = bell_draw(splits[2], (D, 3, HEADS * HEAD_DIM), D ** -0.5, 0.078125, ((2, 32),))
    up_weight = bell_draw(splits[3], (D, FF), D ** -0.5, 0.078125, ((1, 32),))
    proj_weight = bell_draw(splits[4], (HEADS * HEAD_DIM, D), (HEADS * HEAD_DIM) ** -0.5, 0.09375, ((0, 32),))
    down_weight = bell_draw(splits[5], (FF, D), FF ** -0.5, 0.0546875, ((0, 32),))
    query_gain = jnp.clip(1.0 + 0.18 * jax.random.normal(splits[6], (HEAD_DIM,), jnp.float32), 0.1, 1.9)
    key_gain = jnp.clip(1.0 + 0.18 * jax.random.normal(splits[7], (HEAD_DIM,), jnp.float32), 0.1, 1.9)
    out_grad = bell_draw(splits[8], (TOKENS, D), 1.0, 6.0, ((0, 128),))
    return dict(tokens=tokens, norm_gain=norm_gain, qkv_weight=qkv_weight, up_weight=up_weight, proj_weight=proj_weight, down_weight=down_weight, query_gain=query_gain, key_gain=key_gain, out_grad=out_grad)


def head_norm(hidden, gain):
    factor = lax.rsqrt(lax.optimization_barrier(jnp.mean(hidden * hidden, axis=-1, keepdims=True)) + 1e-06)
    return (hidden * factor * gain).astype(jnp.bfloat16)

def attend_mix(hidden_qkv, hidden_up, query_gain, key_gain):
    row_count = hidden_qkv.shape[0]
    head_count = hidden_qkv.shape[2]
    head_size = hidden_qkv.shape[3]
    grid_shape = (row_count // PATCHES, PATCHES, head_count, head_size)
    queries = head_norm(hidden_qkv[:, 0], query_gain).reshape(grid_shape)
    keys_normed = head_norm(hidden_qkv[:, 1], key_gain).reshape(grid_shape)
    values_cast = hidden_qkv[:, 2].astype(jnp.bfloat16).reshape(grid_shape)
    scores = jnp.einsum('ithe,ishe->ihts', queries.astype(jnp.float32), keys_normed.astype(jnp.float32)) * head_size ** (-0.5)
    weights = jnp.exp(scores)
    probs = (weights / lax.optimization_barrier(jnp.sum(weights, axis=-1, keepdims=True))).astype(jnp.bfloat16)
    attended = jnp.einsum('ihts,ishe->ithe', probs.astype(jnp.float32), values_cast.astype(jnp.float32))
    attended = attended.reshape(row_count, head_count * head_size).astype(jnp.bfloat16)
    activated = jax.nn.gelu(hidden_up, approximate=True).astype(jnp.bfloat16)
    return (attended, activated)

def contract_last(left, right):
    return lax.dot_general(left, right, (((1,), (1,)), ((), ())), preferred_element_type=jnp.float32)

def contract_first(left, right):
    return lax.dot_general(left, right, (((0,), (0,)), ((), ())), preferred_element_type=jnp.float32)

def reference(tokens, norm_gain, qkv_weight, up_weight, proj_weight, down_weight, query_gain, key_gain, out_grad):
    token_float = tokens.astype(jnp.float32)
    scale = lax.rsqrt(lax.optimization_barrier(jnp.mean(token_float * token_float, axis=1, keepdims=True)) + 1e-06)
    normed = (token_float * scale * norm_gain).astype(jnp.bfloat16)
    width_qkv = 3 * HEADS * HEAD_DIM
    qkv_flat = qkv_weight.reshape(D, width_qkv)
    hidden_qkv = jnp.dot(normed, qkv_flat, preferred_element_type=jnp.float32).reshape(TOKENS, 3, HEADS, HEAD_DIM)
    hidden_up = jnp.dot(normed, up_weight, preferred_element_type=jnp.float32)
    (attended, activated), pullback = jax.vjp(attend_mix, hidden_qkv, hidden_up, query_gain, key_gain)
    attended_grad = contract_last(out_grad, proj_weight).astype(jnp.bfloat16)
    activated_grad = contract_last(out_grad, down_weight).astype(jnp.bfloat16)
    qkv_cot, up_cot, query_cot, key_cot = pullback((attended_grad, activated_grad))
    hidden_grad = jnp.concatenate([qkv_cot.reshape(TOKENS, width_qkv), up_cot], axis=1).astype(jnp.bfloat16)
    normed_grad = contract_last(hidden_grad[:, :width_qkv], qkv_flat) + contract_last(hidden_grad[:, width_qkv:], up_weight)
    scaled = normed_grad * norm_gain
    inner_mean = lax.optimization_barrier(jnp.mean(scaled * token_float, axis=1, keepdims=True))
    token_grad = (out_grad.astype(jnp.float32) + scale * scaled - token_float * scale * scale * scale * inner_mean).astype(jnp.bfloat16)
    norm_gain_grad = lax.optimization_barrier(jnp.sum(normed_grad * token_float * scale, axis=0))
    qk_gain_grad = jnp.stack([query_cot, key_cot])
    active = jnp.concatenate([attended, activated], axis=1)
    group_rows = IMG_DEV * PATCHES
    grad_in = jnp.zeros((D, hidden_grad.shape[1]), jnp.float32)
    grad_out = jnp.zeros((D, active.shape[1]), jnp.float32)
    for group_index in range(TOKENS // group_rows):
        first_row = group_index * group_rows
        last_row = first_row + group_rows
        part_in = contract_first(normed[first_row:last_row], hidden_grad[first_row:last_row]).astype(jnp.bfloat16)
        part_out = contract_first(out_grad[first_row:last_row], active[first_row:last_row]).astype(jnp.bfloat16)
        part_in, part_out = lax.optimization_barrier((part_in, part_out))
        grad_in = grad_in + part_in.astype(jnp.float32)
        grad_out = grad_out + part_out.astype(jnp.float32)
    width_attn = HEADS * HEAD_DIM
    qkv_grad = grad_in[:, :width_qkv].reshape(D, 3, width_attn)
    up_grad = grad_in[:, width_qkv:]
    proj_grad = grad_out[:, :width_attn].T
    down_grad = grad_out[:, width_attn:].T
    return (token_grad, norm_gain_grad, qk_gain_grad, qkv_grad, up_grad, proj_grad, down_grad)
```

```python
import jax
import jax.numpy as jnp
from jax import lax
from jax.experimental import pallas as pl
from jax.experimental.pallas import tpu as pltpu
from jax.sharding import PartitionSpec as P

F32, BF16 = jnp.float32, jnp.bfloat16
MESH = pl.DeviceIdType.MESH

D = 6144
HALF = D // 2
QUART = D // 4
PATCHES = 256
HEAD = 128
UP = 384
W_IN = 3 * HEAD + UP
W_OUT = HEAD + UP
ROWS = 16
TILE = 256
PART = (slice(0, HALF // 2), slice(HALF // 2, HALF))
EPS = 1e-06
GELU_A, GELU_B = 0.7978845608028654, 0.044715


def dot(left, right, dims):
    return lax.dot_general(left, right, (dims, ((), ())), preferred_element_type=F32)


def kernel(
    tok_ref, og_ref, gain_ref, qg_ref, kg_ref, wqkv_ref, wup_ref, wproj_ref, wdown_ref,
    tg_ref, gsum_ref, dqkv_ref, dup_ref, dout_ref,
    nrm, N, C, G, win, wout, XS, XR, H, HG, ACT, FB1, MB1, FB2, MB2, FS, MS, YR,
    SD, RD, SO, RO, GS, GQ, GC, GY, GX, GZ,
    wsem, y_s, y_r, ag_s, ag_r, e_s, e_r, rs_s, rs_r, z_s, z_r, d_s, d_r, g_s, g_r,
):
    dp, mp = lax.axis_index("dp"), lax.axis_index("mp")
    y_hi, core = dp // 2, dp % 2
    y_lo, x, z = mp // 16, (mp // 4) % 4, mp % 4
    y = y_hi * 2 + y_lo

    def dev(dx=0, dy=0, dz=0, dc=0):
        xx, yy, zz, cc = (x + dx) % 4, (y + dy) % 4, (z + dz) % 4, (core + dc) % 2
        return ((yy // 2) * 2 + cc, (yy % 2) * 16 + xx * 4 + zz)

    def copy(src, dst, send, recv, to):
        return pltpu.make_async_remote_copy(
            src_ref=src, dst_ref=dst, send_sem=send, recv_sem=recv, device_id=to, device_id_type=MESH
        )

    pending = []

    def send(*args):
        cp = copy(*args)
        cp.start()
        pending.append(cp)
        return cp

    half = pl.ds(pl.multiple_of(y_hi * HALF, HALF), HALF)
    loads = [
        pltpu.make_async_copy(wqkv_ref.at[j, half], win.at[:, pl.ds(j * HEAD, HEAD)], wsem.at[j])
        for j in range(3)
    ]
    loads.append(pltpu.make_async_copy(wup_ref.at[half], win.at[:, pl.ds(3 * HEAD, UP)], wsem.at[3]))
    loads.append(pltpu.make_async_copy(wproj_ref.at[:, half], wout.at[pl.ds(0, HEAD)], wsem.at[4]))
    loads.append(pltpu.make_async_copy(wdown_ref.at[:, half], wout.at[pl.ds(HEAD, UP)], wsem.at[5]))
    for cp in loads:
        cp.start()

    barrier = pltpu.get_barrier_semaphore()
    peers = [dev(dy=d) for d in (1, 2, 3)] + [dev(dx=d) for d in (1, 2, 3)]
    peers += [dev(dz=d) for d in (1, 2, 3)] + [dev(dc=1)]
    for peer in peers:
        pl.semaphore_signal(barrier, inc=1, device_id=peer, device_id_type=MESH)

    tok = tok_ref[...].astype(F32)
    scale = lax.rsqrt(jnp.mean(tok * tok, axis=1, keepdims=True) + EPS)
    nrm[...] = (tok * scale * gain_ref[...]).astype(BF16)
    zrow = pl.ds(pl.multiple_of(z * ROWS, ROWS), ROWS)
    N[y_lo, y_hi, x, zrow, :] = nrm[:, half]
    C[y_lo, y_hi, x, zrow, :] = og_ref[:, half]
    GS[...] = jnp.zeros_like(GS)
    GQ[...] = jnp.zeros_like(GQ)
    pl.semaphore_wait(barrier, len(peers))

    y_copies = []
    for a, (src, dst) in enumerate(((nrm, N), (og_ref, C))):
        row = []
        for dy in (1, 2, 3):
            there = ((y + dy) % 4) // 2
            cols = pl.ds(pl.multiple_of(there * HALF, HALF), HALF)
            row.append(
                send(src.at[:, cols], dst.at[y_lo, y_hi, x, zrow, :],
                     y_s.at[a, dy - 1], y_r.at[a, dy - 1], dev(dy=dy))
            )
        y_copies.append(row)

    def zr(i):
        return pl.ds(pl.multiple_of(((z + i) % 4) * ROWS, ROWS), ROWS)

    def ag_first(ref, k, p, off, yh):
        if p == 0:
            return ref.at[k, yh, (x + off) % 4, zrow, PART[0]]
        return ref.at[k, yh, x, zr(off), PART[1]]

    def ag_second(ref, k, p, off, yh):
        if p == 0:
            return ref.at[k, yh, :, zr(off), PART[0]]
        return ref.at[k, yh, (x + off) % 4, :, PART[1]]

    def ag_dev(p, phase, step):
        return dev(dx=step) if p == phase else dev(dz=step)

    units = [(N, 0), (C, 0), (N, 1), (C, 1)]
    ag = {}

    def ag_own(u, phase):
        ref, k = units[u]
        where = (ag_first, ag_second)[phase]
        for p in (0, 1):
            for d, step in enumerate((1, -1)):
                block = where(ref, k, p, 0, slice(None))
                ag[u, phase, 0, p, d] = send(
                    block, block, ag_s.at[u, phase, p, d], ag_r.at[u, phase, p, d], ag_dev(p, phase, step)
                )

    def ag_fwd(u, phase):
        ref, k = units[u]
        where = (ag_first, ag_second)[phase]
        for p in (0, 1):
            for d, step in enumerate((1, -1)):
                ag[u, phase, 0, p, d].wait_recv()
                block = where(ref, k, p, -step, d)
                ag[u, phase, 1, p, d] = send(
                    block, block, ag_s.at[u, phase, p, 2 + d], ag_r.at[u, phase, p, 2 + d],
                    ag_dev(p, phase, step),
                )

    def ag_end(u, phase):
        for p in (0, 1):
            for d in (0, 1):
                ag[u, phase, 1, p, d].wait_recv()

    partner = dev(dy=2)

    def rows_of(ref, k, yh):
        return ref[k, yh].reshape(PATCHES, HALF)

    def partial_in(k):
        other = 1 - y_hi

        @pl.loop(0, W_IN // TILE)
        def _(j):
            cols = pl.ds(pl.multiple_of(j * TILE, TILE), TILE)
            XS[k, :, cols] = dot(rows_of(N, k, other), win[:, cols], ((1,), (0,))).astype(BF16)

        cp = send(XS.at[k, :, pl.ds(0, W_IN)], XR.at[k, :, pl.ds(0, W_IN)], e_s.at[k, 0], e_r.at[k, 0], partner)

        @pl.loop(0, W_IN // TILE)
        def _(j):
            cols = pl.ds(pl.multiple_of(j * TILE, TILE), TILE)
            H[k, :, cols] = dot(rows_of(N, k, y_hi), win[:, cols], ((1,), (0,)))

        return cp

    def partial_out(k):
        other = 1 - y_hi

        @pl.loop(0, W_OUT // TILE)
        def _(j):
            rows = pl.ds(pl.multiple_of(j * TILE, TILE), TILE)
            cols = pl.ds(pl.multiple_of(W_IN + j * TILE, TILE), TILE)
            XS[k, :, cols] = dot(rows_of(C, k, other), wout[rows, :], ((1,), (1,))).astype(BF16)

        cp = send(XS.at[k, :, pl.ds(W_IN, W_OUT)], XR.at[k, :, pl.ds(W_IN, W_OUT)],
                  e_s.at[k, 1], e_r.at[k, 1], partner)

        @pl.loop(0, W_OUT // TILE)
        def _(j):
            rows = pl.ds(pl.multiple_of(j * TILE, TILE), TILE)
            cols = pl.ds(pl.multiple_of(W_IN + j * TILE, TILE), TILE)
            H[k, :, cols] = dot(rows_of(C, k, y_hi), wout[rows, :], ((1,), (1,)))

        return cp

    def summed(k, start, width, rows=slice(None)):
        cols = pl.ds(start, width)
        return H[k, rows, cols] + XR[k, rows, cols].astype(F32)

    def head_norm(h, g):
        factor = lax.rsqrt(jnp.mean(h * h, axis=1, keepdims=True) + EPS)
        return factor, (h * factor * g).astype(BF16)

    def head_norm_back(h, factor, g, dy):
        hf = h * factor
        dyg = dy * g
        dh = factor * (dyg - hf * jnp.mean(hf * dyg, axis=1, keepdims=True))
        return dh, jnp.sum(dy * hf, axis=0, keepdims=True)

    def middle(k):
        hq, hk = summed(k, 0, HEAD), summed(k, HEAD, HEAD)
        v = summed(k, 2 * HEAD, HEAD).astype(BF16)
        da = summed(k, W_IN, HEAD).astype(BF16)
        qg, kg = qg_ref[...], kg_ref[...]
        fq, qn = head_norm(hq, qg)
        fk, kn = head_norm(hk, kg)
        w = jnp.exp(dot(qn, kn, ((1,), (1,))) * HEAD**-0.5)
        probs = w / jnp.sum(w, axis=1, keepdims=True)
        probs_b = probs.astype(BF16)
        ACT[k, y_hi, :, 0:HEAD] = dot(probs_b, v, ((1,), (0,))).astype(BF16)
        dpr = dot(da, v, ((1,), (1,))).astype(BF16).astype(F32)
        HG[k, y_hi, :, 2 * HEAD : 3 * HEAD] = dot(probs_b, da, ((0,), (0,))).astype(BF16)
        ds = probs * (dpr - jnp.sum(probs * dpr, axis=1, keepdims=True))
        ds = (ds * HEAD**-0.5).astype(BF16)
        dqn = dot(ds, kn, ((1,), (0,))).astype(BF16).astype(F32)
        dkn = dot(ds, qn, ((0,), (0,))).astype(BF16).astype(F32)
        dhq, dqg = head_norm_back(hq, fq, qg, dqn)
        dhk, dkg = head_norm_back(hk, fk, kg, dkn)
        HG[k, y_hi, :, 0:HEAD] = dhq.astype(BF16)
        HG[k, y_hi, :, HEAD : 2 * HEAD] = dhk.astype(BF16)
        GQ[0:1, :] += dqg
        GQ[1:2, :] += dkg

        @pl.loop(0, 4)
        def _(i):
            rows = pl.ds(pl.multiple_of(i * 64, 64), 64)
            u = summed(k, 3 * HEAD, UP, rows)
            dact = summed(k, W_IN + HEAD, UP, rows).astype(BF16).astype(F32)
            t = jnp.tanh(GELU_A * (u + GELU_B * (u * u * u)))
            ACT[k, y_hi, rows, HEAD:] = (0.5 * u * (1.0 + t)).astype(BF16)
            slope = 0.5 * (1.0 + t) + 0.5 * u * (1.0 - t * t) * (GELU_A * (1.0 + 3.0 * GELU_B * (u * u)))
            HG[k, y_hi, rows, 3 * HEAD :] = (dact * slope).astype(BF16)

        return (
            send(HG.at[k, y_hi], HG.at[k, y_hi], e_s.at[k, 2], e_r.at[k, 2], partner),
            send(ACT.at[k, y_hi], ACT.at[k, y_hi], e_s.at[k, 3], e_r.at[k, 3], partner),
        )

    def normed_grad(k, yh):
        @pl.loop(0, HALF // TILE)
        def _(j):
            cols = pl.ds(pl.multiple_of(j * TILE, TILE), TILE)
            ng = dot(HG[k, yh], win[cols, :], ((1,), (1,)))
            G[k, yh, :, :, cols] = ng.astype(BF16).reshape(4, 64, TILE)
            term = ng * N[k, yh, :, :, cols].reshape(PATCHES, TILE).astype(F32)
            GS[:, cols] += jnp.sum(term.reshape(PATCHES // 8, 8, TILE), axis=0)

    def rs_bufs(k, phase, p):
        if phase == 1:
            return (FB1, FB2)[p].at[k], (MB1, MB2)[p].at[k]
        return FS.at[p, k], MS.at[p, k]

    rs = {}

    def rs_start(k, phase):
        where = (ag_first, ag_second)[phase]
        for p in (0, 1):
            fr, mr = rs_bufs(k, phase, p)
            for d, step in enumerate((1, -1)):
                to = ag_dev(p, phase, step)
                sems = lambda i: (rs_s.at[k, phase, p, d, i], rs_r.at[k, phase, p, d, i])
                rs[k, phase, p, d, 0] = send(where(G, k, p, 2, d), fr.at[d], *sems(0), to)
                rs[k, phase, p, d, 1] = send(where(G, k, p, step, 1 - d), mr.at[d, 1 - d], *sems(1), to)

    def rs_mid(k, phase):
        where = (ag_first, ag_second)[phase]
        for p in (0, 1):
            fr, mr = rs_bufs(k, phase, p)
            for d, step in enumerate((1, -1)):
                to = ag_dev(p, phase, step)
                rs[k, phase, p, d, 0].wait_recv()
                block = where(G, k, p, step, d)
                block[...] = (block[...].astype(F32) + fr[d].astype(F32)).astype(BF16)
                rs[k, phase, p, d, 2] = send(
                    block, mr.at[d, d], rs_s.at[k, phase, p, d, 2], rs_r.at[k, phase, p, d, 2], to
                )

    def rs_end(k, phase):
        where = (ag_first, ag_second)[phase]
        for p in (0, 1):
            _, mr = rs_bufs(k, phase, p)
            for d in (0, 1):
                rs[k, phase, p, d, 1].wait_recv()
                rs[k, phase, p, d, 2].wait_recv()
            for yh in (0, 1):
                block = where(G, k, p, 0, yh)
                total = block[...].astype(F32) + mr[0, yh].astype(F32) + mr[1, yh].astype(F32)
                block[...] = total.astype(BF16)

    def feature_tile(t, whose):
        return pl.ds(pl.multiple_of(whose * QUART + t * TILE, TILE), TILE)

    def grad_in(t, whose):
        left = N[:, :, :, :, feature_tile(t, whose)].reshape(4 * PATCHES, TILE)
        return dot(left, HG[...].reshape(4 * PATCHES, W_IN), ((0,), (0,)))

    def grad_out(t, whose):
        right = C[:, :, :, :, feature_tile(t, whose)].reshape(4 * PATCHES, TILE)
        return dot(ACT[...].reshape(4 * PATCHES, W_OUT), right, ((0,), (0,)))

    def swap(kind, t):
        src, dst = ((SD, RD), (SO, RO))[kind]
        return copy(src.at[t], dst.at[t], d_s.at[kind, t], d_r.at[kind, t], dev(dc=1))

    tiles = QUART // TILE

    def grads_away():
        @pl.loop(0, tiles)
        def _(t):
            SD[t] = grad_in(t, 1 - core).astype(BF16)
            swap(0, t).start()

        @pl.loop(0, tiles)
        def _(t):
            SO[t] = grad_out(t, 1 - core).astype(BF16)
            swap(1, t).start()

    def grads_in_here():
        @pl.loop(0, tiles)
        def _(t):
            own = grad_in(t, core)
            swap(0, t).wait_recv()
            rows = pl.ds(pl.multiple_of(t * TILE, TILE), TILE)
            total = own + RD[t].astype(F32)
            for j in range(3):
                dqkv_ref[j, rows, :] = total[:, j * HEAD : (j + 1) * HEAD].astype(BF16)
            dup_ref[rows, :] = total[:, 3 * HEAD :].astype(BF16)

    def grads_out_here():
        @pl.loop(0, tiles)
        def _(t):
            own = grad_out(t, core)
            swap(1, t).wait_recv()
            cols = pl.ds(pl.multiple_of(t * TILE, TILE), TILE)
            dout_ref[:, cols] = (own + RO[t].astype(F32)).astype(BF16)

    def gain_send(stage, slots, me, tos):
        return [
            send(slots.at[me], slots.at[me], g_s.at[stage, i], g_r.at[stage, i], to)
            for i, to in enumerate(tos)
        ]

    def wait_all(cps):
        for cp in cps:
            cp.wait_recv()

    wait_all(y_copies[0])
    ag_own(0, 0)
    wait_all(y_copies[1])
    ag_own(1, 0)
    ag_fwd(0, 0)
    ag_end(0, 0)
    ag_own(0, 1)
    ag_fwd(1, 0)
    ag_end(1, 0)
    ag_own(1, 1)
    ag_own(2, 0)
    for cp in loads:
        cp.wait()
    ag_fwd(0, 1)
    ag_fwd(2, 0)
    ag_end(2, 0)
    ag_own(2, 1)
    ag_own(3, 0)
    ag_end(0, 1)
    e_in0 = partial_in(0)
    ag_fwd(1, 1)
    ag_fwd(3, 0)
    ag_end(3, 0)
    ag_own(3, 1)
    ag_end(1, 1)
    e_out0 = partial_out(0)
    ag_fwd(2, 1)
    wait_all((e_in0, e_out0))
    back0 = middle(0)
    ag_end(2, 1)
    e_in1 = partial_in(1)
    ag_fwd(3, 1)
    normed_grad(0, y_hi)
    wait_all(back0)
    normed_grad(0, 1 - y_hi)
    rs_start(0, 1)
    ag_end(3, 1)
    e_out1 = partial_out(1)
    rs_mid(0, 1)
    wait_all((e_in1, e_out1))
    back1 = middle(1)
    rs_end(0, 1)
    rs_start(0, 0)
    normed_grad(1, y_hi)
    rs_mid(0, 0)
    wait_all(back1)
    normed_grad(1, 1 - y_hi)
    rs_start(1, 1)
    rs_end(0, 0)
    gsum = jnp.sum(GS[...], axis=0, keepdims=True)
    for j in range(HALF // HEAD):
        GC[core, j : j + 1, :] = gsum[:, j * HEAD : (j + 1) * HEAD]
    GC[core, 24:32, :] = GQ[...]
    g0 = gain_send(0, GC, core, [dev(dc=1)])
    grads_away()
    rs_mid(1, 1)
    wait_all(g0)
    GY[y] = GC[0] + GC[1]
    g1 = gain_send(1, GY, y, [dev(dy=d) for d in (1, 2, 3)])
    grads_in_here()
    rs_end(1, 1)
    rs_start(1, 0)
    wait_all(g1)
    GX[x, 0] = GY[0] + GY[1]
    GX[x, 1] = GY[2] + GY[3]
    g2 = gain_send(2, GX, x, [dev(dx=d) for d in (1, 2, 3)])
    rs_mid(1, 0)
    grads_out_here()
    rs_end(1, 0)

    last = []
    for dy in (1, 2, 3):
        yy = (y + dy) % 4
        last.append(
            send(G.at[yy % 2, yy // 2, x, zrow, :], YR.at[y], z_s.at[dy - 1], z_r.at[dy - 1], dev(dy=dy))
        )
    YR[y] = G[y_lo, y_hi, x, zrow, :]
    wait_all(g2)
    GZ[z] = ((GX[0] + GX[1]) + GX[2]) + GX[3]
    g3 = gain_send(3, GZ, z, [dev(dz=d) for d in (1, 2, 3)])
    wait_all(last)
    inner = jnp.zeros((ROWS, 1), F32)
    for h in (0, 1):
        cols = slice(h * HALF, (h + 1) * HALF)
        c = (YR[2 * h].astype(F32) + YR[2 * h + 1].astype(F32)) * gain_ref[:, cols]
        inner += jnp.sum(c * tok_ref[:, cols].astype(F32), axis=1, keepdims=True)
    inner = inner / D
    for h in (0, 1):
        cols = slice(h * HALF, (h + 1) * HALF)
        c = (YR[2 * h].astype(F32) + YR[2 * h + 1].astype(F32)) * gain_ref[:, cols]
        own = tok_ref[:, cols].astype(F32)
        grad = og_ref[:, cols].astype(F32) + scale * c - own * (scale * scale * scale * inner)
        tg_ref[:, cols] = grad.astype(BF16)
    wait_all(g3)
    gsum_ref[...] = ((GZ[0] + GZ[1]) + GZ[2]) + GZ[3]

    for cp in pending:
        cp.wait_send()

    @pl.loop(0, tiles)
    def _(t):
        swap(0, t).wait_send()
        swap(1, t).wait_send()


def per_device(tokens, norm_gain, qkv_weight, up_weight, proj_weight, down_weight, query_gain, key_gain, out_grad):
    vm, hbm = pl.BlockSpec(memory_space=pltpu.VMEM), pl.BlockSpec(memory_space=pl.ANY)
    tiles = QUART // TILE
    quarter = HALF // 2
    dma = pltpu.SemaphoreType.DMA
    scratch = [
        pltpu.VMEM((ROWS, D), BF16),
        pltpu.VMEM((2, 2, 4, 64, HALF), BF16),
        pltpu.VMEM((2, 2, 4, 64, HALF), BF16),
        pltpu.VMEM((2, 2, 4, 64, HALF), BF16),
        pltpu.VMEM((HALF, W_IN), BF16),
        pltpu.VMEM((W_OUT, HALF), BF16),
        pltpu.VMEM((2, PATCHES, W_IN + W_OUT), BF16),
        pltpu.VMEM((2, PATCHES, W_IN + W_OUT), BF16),
        pltpu.VMEM((2, PATCHES, W_IN + W_OUT), F32),
        pltpu.VMEM((2, 2, PATCHES, W_IN), BF16),
        pltpu.VMEM((2, 2, PATCHES, W_OUT), BF16),
        pltpu.VMEM((2, 2, 4, ROWS, quarter), BF16),
        pltpu.VMEM((2, 2, 2, 4, ROWS, quarter), BF16),
        pltpu.VMEM((2, 2, 64, quarter), BF16),
        pltpu.VMEM((2, 2, 2, 64, quarter), BF16),
        pltpu.VMEM((2, 2, 2, ROWS, quarter), BF16),
        pltpu.VMEM((2, 2, 2, 2, ROWS, quarter), BF16),
        pltpu.VMEM((4, ROWS, HALF), BF16),
        pltpu.VMEM((tiles, TILE, W_IN), BF16),
        pltpu.VMEM((tiles, TILE, W_IN), BF16),
        pltpu.VMEM((tiles, W_OUT, TILE), BF16),
        pltpu.VMEM((tiles, W_OUT, TILE), BF16),
        pltpu.VMEM((8, HALF), F32),
        pltpu.VMEM((8, HEAD), F32),
        pltpu.VMEM((2, 32, HEAD), F32),
        pltpu.VMEM((4, 32, HEAD), F32),
        pltpu.VMEM((4, 2, 32, HEAD), F32),
        pltpu.VMEM((4, 2, 32, HEAD), F32),
        dma((6,)),
        dma((2, 3)),
        dma((2, 3)),
        dma((4, 2, 2, 4)),
        dma((4, 2, 2, 4)),
        dma((2, 4)),
        dma((2, 4)),
        dma((2, 2, 2, 2, 3)),
        dma((2, 2, 2, 2, 3)),
        dma((3,)),
        dma((3,)),
        dma((2, tiles)),
        dma((2, tiles)),
        dma((4, 3)),
        dma((4, 3)),
    ]
    token_grad, gains, dqkv, dup, dout = pl.pallas_call(
        kernel,
        name="block",
        out_shape=(
            jax.ShapeDtypeStruct((ROWS, D), BF16),
            jax.ShapeDtypeStruct((2, 32, HEAD), F32),
            jax.ShapeDtypeStruct((3, QUART, HEAD), BF16),
            jax.ShapeDtypeStruct((QUART, UP), BF16),
            jax.ShapeDtypeStruct((W_OUT, QUART), BF16),
        ),
        in_specs=[vm] * 5 + [hbm] * 4,
        out_specs=(vm,) * 5,
        scratch_shapes=scratch,
        compiler_params=pltpu.CompilerParams(
            collective_id=0, has_side_effects=True, vmem_limit_bytes=60 * 1024 * 1024
        ),
        cost_estimate=pl.CostEstimate(flops=21 * 10**9, bytes_accessed=20 * 10**6, transcendentals=0),
    )(
        tokens, out_grad, norm_gain.reshape(1, D), query_gain.reshape(1, HEAD), key_gain.reshape(1, HEAD),
        jnp.transpose(qkv_weight, (1, 0, 2)), up_weight, proj_weight, down_weight,
    )
    norm_gain_grad = gains[:, : HALF // HEAD].reshape(D) / norm_gain
    qk_gain_grad = gains[0, 24:26] + gains[1, 24:26]
    return (
        token_grad,
        norm_gain_grad,
        qk_gain_grad,
        jnp.transpose(dqkv, (1, 0, 2)).astype(F32),
        dup.astype(F32),
        dout[:HEAD].astype(F32),
        dout[HEAD:].astype(F32),
    )


def solution(mesh):
    rows = P(("dp", "mp"), None)
    placed = (rows, P(), P(None, None, "mp"), P(None, "mp"), P("mp", None), P("mp", None), P(), P(), rows)
    outs = (rows, P(), P(), P("dp", None, "mp"), P("dp", "mp"), P("mp", "dp"), P("mp", "dp"))
    return jax.shard_map(per_device, mesh=mesh, in_specs=placed, out_specs=outs, check_vma=False)
```

```python
import jax
import jax.numpy as jnp
from jax import lax
from jax.experimental import pallas as pl
from jax.experimental.pallas import tpu as pltpu
from jax.sharding import PartitionSpec as P

F32, BF16 = jnp.float32, jnp.bfloat16
MESH = pl.DeviceIdType.MESH

D = 6144
HALF = D // 2
QUART = D // 4
PATCHES = 256
HEAD = 128
UP = 384
W_IN = 3 * HEAD + UP
W_OUT = HEAD + UP
ROWS = 16
TILE = 256
WIDE = 512
PART = (slice(0, HALF // 2), slice(HALF // 2, HALF))
EPS = 1e-06
GELU_A, GELU_B = 0.7978845608028654, 0.044715


def dot(left, right, dims):
    return lax.dot_general(left, right, (dims, ((), ())), preferred_element_type=F32)


def kernel(
    tok_ref, og_ref, gain_ref, gain_rows_ref, qg_ref, kg_ref, wqkv_ref, wup_ref, wproj_ref, wdown_ref,
    tg_ref, gsum_ref, qk_ref, dqkv_ref, dup_ref, dproj_ref, ddown_ref,
    nrm, N, C, G, win, wout, XS, XR, H, HG, ACT, FB1, MB1, FB2, MB2, FS, MS, YR,
    SD, RD, SO, RO, GS, GQ, GC, GY, GX, GZ,
    wsem, y_s, y_r, ag_s, ag_r, e_s, e_r, rs_s, rs_r, z_s, z_r, d_s, d_r, g_s, g_r,
):
    dp, mp = lax.axis_index("dp"), lax.axis_index("mp")
    y_hi, core = dp // 2, dp % 2
    y_lo, x, z = mp // 16, (mp // 4) % 4, mp % 4
    y = y_hi * 2 + y_lo

    def dev(dx=0, dy=0, dz=0, dc=0):
        xx, yy, zz, cc = (x + dx) % 4, (y + dy) % 4, (z + dz) % 4, (core + dc) % 2
        return ((yy // 2) * 2 + cc, (yy % 2) * 16 + xx * 4 + zz)

    def copy(src, dst, send, recv, to):
        return pltpu.make_async_remote_copy(
            src_ref=src, dst_ref=dst, send_sem=send, recv_sem=recv, device_id=to, device_id_type=MESH
        )

    pending = []

    def send(*args):
        cp = copy(*args)
        cp.start()
        pending.append(cp)
        return cp

    half = pl.ds(pl.multiple_of(y_hi * HALF, HALF), HALF)
    loads = [
        pltpu.make_async_copy(wqkv_ref.at[j, half], win.at[:, pl.ds(j * HEAD, HEAD)], wsem.at[j])
        for j in range(3)
    ]
    loads.append(pltpu.make_async_copy(wup_ref.at[half], win.at[:, pl.ds(3 * HEAD, UP)], wsem.at[3]))
    loads.append(pltpu.make_async_copy(wproj_ref.at[:, half], wout.at[pl.ds(0, HEAD)], wsem.at[4]))
    loads.append(pltpu.make_async_copy(wdown_ref.at[:, half], wout.at[pl.ds(HEAD, UP)], wsem.at[5]))
    for cp in loads:
        cp.start()

    barrier = pltpu.get_barrier_semaphore()
    peers = [dev(dy=d) for d in (1, 2, 3)] + [dev(dx=d) for d in (1, 2, 3)]
    peers += [dev(dz=d) for d in (1, 2, 3)] + [dev(dc=1)]
    for peer in peers:
        pl.semaphore_signal(barrier, inc=1, device_id=peer, device_id_type=MESH)

    zrow = pl.ds(pl.multiple_of(z * ROWS, ROWS), ROWS)

    tok = tok_ref[...].astype(F32)
    scale = lax.rsqrt(jnp.mean(tok * tok, axis=1, keepdims=True) + EPS)
    nrm[...] = (tok * scale * gain_ref[...]).astype(BF16)
    N[y_lo, y_hi, x, zrow, :] = nrm[:, half]
    C[y_lo, y_hi, x, zrow, :] = og_ref[:, half]
    pl.semaphore_wait(barrier, len(peers))

    def along_y(a, src, dst):
        row = []
        for dy in (1, 2, 3):
            there = ((y + dy) % 4) // 2
            cols = pl.ds(pl.multiple_of(there * HALF, HALF), HALF)
            row.append(
                send(src.at[:, cols], dst.at[y_lo, y_hi, x, zrow, :],
                     y_s.at[a, dy - 1], y_r.at[a, dy - 1], dev(dy=dy))
            )
        return row

    y_in = along_y(0, nrm, N)
    y_out = along_y(1, og_ref, C)
    GS[...] = jnp.zeros_like(GS)
    GQ[...] = jnp.zeros_like(GQ)

    def zr(i):
        return pl.ds(pl.multiple_of(((z + i) % 4) * ROWS, ROWS), ROWS)

    def ag_first(ref, k, p, off, yh):
        if p == 0:
            return ref.at[k, yh, (x + off) % 4, zrow, PART[0]]
        return ref.at[k, yh, x, zr(off), PART[1]]

    def ag_second(ref, k, p, off, yh):
        if p == 0:
            return ref.at[k, yh, :, zr(off), PART[0]]
        return ref.at[k, yh, (x + off) % 4, :, PART[1]]

    def ag_dev(p, phase, step):
        return dev(dx=step) if p == phase else dev(dz=step)

    units = [(N, 0), (C, 0), (N, 1), (C, 1)]
    ag = {}

    def ag_own(u, phase):
        ref, k = units[u]
        where = (ag_first, ag_second)[phase]
        for first in (0, 1):
            for p in (0, 1):
                for d, step in enumerate((1, -1)):
                    yh = d if first == 0 else 1 - d
                    block = where(ref, k, p, 0, yh)
                    ag[u, phase, first, p, d] = send(
                        block, block, ag_s.at[u, phase, p, d, first], ag_r.at[u, phase, p, d, first],
                        ag_dev(p, phase, step),
                    )

    def ag_fwd(u, phase):
        ref, k = units[u]
        where = (ag_first, ag_second)[phase]
        for p in (0, 1):
            for d, step in enumerate((1, -1)):
                ag[u, phase, 0, p, d].wait_recv()
                block = where(ref, k, p, -step, d)
                ag[u, phase, 2, p, d] = send(
                    block, block, ag_s.at[u, phase, p, d, 2], ag_r.at[u, phase, p, d, 2],
                    ag_dev(p, phase, step),
                )

    def ag_wait(u, phase, i):
        for p in (0, 1):
            for d in (0, 1):
                ag[u, phase, i, p, d].wait_recv()

    def ag_end(u, phase):
        if phase == 0:
            ag_wait(u, phase, 1)
        ag_wait(u, phase, 2)

    partner = dev(dy=2)

    def rows_of(ref, k, yh):
        return ref[k, yh].reshape(PATCHES, HALF)

    def partial_in(k):
        other = 1 - y_hi

        @pl.loop(0, W_IN // TILE)
        def _(j):
            cols = pl.ds(pl.multiple_of(j * TILE, TILE), TILE)
            XS[k, :, cols] = dot(rows_of(N, k, other), win[:, cols], ((1,), (0,))).astype(BF16)

        cp = send(XS.at[k, :, pl.ds(0, W_IN)], XR.at[k, :, pl.ds(0, W_IN)], e_s.at[k, 0], e_r.at[k, 0], partner)

        @pl.loop(0, W_IN // TILE)
        def _(j):
            cols = pl.ds(pl.multiple_of(j * TILE, TILE), TILE)
            H[k, :, cols] = dot(rows_of(N, k, y_hi), win[:, cols], ((1,), (0,)))

        return cp

    def partial_out(k):
        other = 1 - y_hi

        @pl.loop(0, W_OUT // TILE)
        def _(j):
            rows = pl.ds(pl.multiple_of(j * TILE, TILE), TILE)
            cols = pl.ds(pl.multiple_of(W_IN + j * TILE, TILE), TILE)
            XS[k, :, cols] = dot(rows_of(C, k, other), wout[rows, :], ((1,), (1,))).astype(BF16)

        cp = send(XS.at[k, :, pl.ds(W_IN, W_OUT)], XR.at[k, :, pl.ds(W_IN, W_OUT)],
                  e_s.at[k, 1], e_r.at[k, 1], partner)

        @pl.loop(0, W_OUT // TILE)
        def _(j):
            rows = pl.ds(pl.multiple_of(j * TILE, TILE), TILE)
            cols = pl.ds(pl.multiple_of(W_IN + j * TILE, TILE), TILE)
            H[k, :, cols] = dot(rows_of(C, k, y_hi), wout[rows, :], ((1,), (1,)))

        return cp

    def summed(k, start, width, rows=slice(None)):
        cols = pl.ds(start, width)
        return H[k, rows, cols] + XR[k, rows, cols].astype(F32)

    def head_norm(h, g):
        factor = lax.rsqrt(jnp.mean(h * h, axis=1, keepdims=True) + EPS)
        return factor, (h * factor * g).astype(BF16)

    def head_norm_back(h, factor, g, dy):
        hf = h * factor
        dyg = dy * g
        dh = factor * (dyg - hf * jnp.mean(hf * dyg, axis=1, keepdims=True))
        return dh, jnp.sum(dy * hf, axis=0, keepdims=True)

    def middle(k):
        hq, hk = summed(k, 0, HEAD), summed(k, HEAD, HEAD)
        v = summed(k, 2 * HEAD, HEAD).astype(BF16)
        da = summed(k, W_IN, HEAD).astype(BF16)
        qg, kg = qg_ref[...], kg_ref[...]
        fq, qn = head_norm(hq, qg)
        fk, kn = head_norm(hk, kg)
        w = jnp.exp(dot(qn, kn, ((1,), (1,))) * HEAD**-0.5)
        probs = w / jnp.sum(w, axis=1, keepdims=True)
        probs_b = probs.astype(BF16)
        ACT[k, y_hi, :, 0:HEAD] = dot(probs_b, v, ((1,), (0,))).astype(BF16)
        dpr = dot(da, v, ((1,), (1,))).astype(BF16).astype(F32)
        HG[k, y_hi, :, 2 * HEAD : 3 * HEAD] = dot(probs_b, da, ((0,), (0,))).astype(BF16)
        ds = probs * (dpr - jnp.sum(probs * dpr, axis=1, keepdims=True))
        ds = (ds * HEAD**-0.5).astype(BF16)
        dqn = dot(ds, kn, ((1,), (0,))).astype(BF16).astype(F32)
        dkn = dot(ds, qn, ((0,), (0,))).astype(BF16).astype(F32)
        dhq, dqg = head_norm_back(hq, fq, qg, dqn)
        dhk, dkg = head_norm_back(hk, fk, kg, dkn)
        HG[k, y_hi, :, 0:HEAD] = dhq.astype(BF16)
        HG[k, y_hi, :, HEAD : 2 * HEAD] = dhk.astype(BF16)
        GQ[0:1, :] += dqg
        GQ[1:2, :] += dkg

        @pl.loop(0, 4)
        def _(i):
            rows = pl.ds(pl.multiple_of(i * 64, 64), 64)
            u = summed(k, 3 * HEAD, UP, rows)
            dact = summed(k, W_IN + HEAD, UP, rows).astype(BF16).astype(F32)
            t = jnp.tanh(GELU_A * (u + GELU_B * (u * u * u)))
            ACT[k, y_hi, rows, HEAD:] = (0.5 * u * (1.0 + t)).astype(BF16)
            slope = 0.5 * (1.0 + t) + 0.5 * u * (1.0 - t * t) * (GELU_A * (1.0 + 3.0 * GELU_B * (u * u)))
            HG[k, y_hi, rows, 3 * HEAD :] = (dact * slope).astype(BF16)

        return send(HG.at[k, y_hi], HG.at[k, y_hi], e_s.at[k, 2], e_r.at[k, 2], partner)

    def swap_act(k):
        return send(ACT.at[k, y_hi], ACT.at[k, y_hi], e_s.at[k, 3], e_r.at[k, 3], partner)

    def normed_grad(k, yh):
        @pl.loop(0, HALF // WIDE)
        def _(j):
            cols = pl.ds(pl.multiple_of(j * WIDE, WIDE), WIDE)
            ng = dot(HG[k, yh], win[cols, :], ((1,), (1,)))
            G[k, yh, :, :, cols] = ng.astype(BF16).reshape(4, 64, WIDE)
            term = ng * N[k, yh, :, :, cols].reshape(PATCHES, WIDE).astype(F32)
            GS[:, cols] += jnp.sum(term.reshape(PATCHES // 8, 8, WIDE), axis=0)

    def rs_bufs(k, phase, p):
        if phase == 1:
            return (FB1, FB2)[p].at[k], (MB1, MB2)[p].at[k]
        return FS.at[p, k], MS.at[p, k]

    rs = {}

    def rs_start(k, phase, yh, tag):
        where = (ag_first, ag_second)[phase]
        step = 1 - 2 * yh
        for p in (0, 1):
            fr, mr = rs_bufs(k, phase, p)
            far, near = where(G, k, p, 2, yh), where(G, k, p, -step, yh)
            sems = [(rs_s.at[k, phase, p, yh, i], rs_r.at[k, phase, p, yh, i]) for i in (0, 1)]
            rs[k, phase, p, tag, 0] = send(far, fr.at[yh], *sems[0], ag_dev(p, phase, step))
            rs[k, phase, p, tag, 1] = send(near, mr.at[1, yh], *sems[1], ag_dev(p, phase, -step))

    def rs_mid(k, phase, yh, tag):
        where = (ag_first, ag_second)[phase]
        step = 1 - 2 * yh
        for p in (0, 1):
            fr, mr = rs_bufs(k, phase, p)
            rs[k, phase, p, tag, 0].wait_recv()
            block = where(G, k, p, step, yh)
            block[...] = (block[...].astype(F32) + fr[yh].astype(F32)).astype(BF16)
            rs[k, phase, p, tag, 2] = send(
                block, mr.at[0, yh], rs_s.at[k, phase, p, yh, 2], rs_r.at[k, phase, p, yh, 2],
                ag_dev(p, phase, step),
            )

    def rs_end(k, phase, yh, tag):
        where = (ag_first, ag_second)[phase]
        for p in (0, 1):
            _, mr = rs_bufs(k, phase, p)
            rs[k, phase, p, tag, 1].wait_recv()
            rs[k, phase, p, tag, 2].wait_recv()
            block = where(G, k, p, 0, yh)
            total = block[...].astype(F32) + mr[0, yh].astype(F32) + mr[1, yh].astype(F32)
            block[...] = total.astype(BF16)

    def feature_tile(t, whose):
        return pl.ds(pl.multiple_of(whose * QUART + t * TILE, TILE), TILE)

    def grad_in(t, whose, k):
        left = N[k, :, :, :, feature_tile(t, whose)].reshape(2 * PATCHES, TILE)
        return dot(left, HG[k].reshape(2 * PATCHES, W_IN), ((0,), (0,)))

    def grad_out(t, whose):
        right = C[:, :, :, :, feature_tile(t, whose)].reshape(4 * PATCHES, TILE)
        return dot(ACT[...].reshape(4 * PATCHES, W_OUT), right, ((0,), (0,)))

    def swap(kind, t):
        src, dst = ((SD, RD), (SO, RO))[kind]
        return copy(src.at[t], dst.at[t], d_s.at[kind, t], d_r.at[kind, t], dev(dc=1))

    tiles = QUART // TILE

    def tile_rows(t):
        return pl.ds(pl.multiple_of(t * TILE, TILE), TILE)

    def keep_in(t, total):
        for j in range(3):
            dqkv_ref[j, tile_rows(t), :] = total[:, j * HEAD : (j + 1) * HEAD].astype(BF16)
        dup_ref[tile_rows(t), :] = total[:, 3 * HEAD :].astype(BF16)

    def in_first():
        @pl.loop(0, tiles)
        def _(t):
            SD[t] = grad_in(t, 1 - core, 0).astype(BF16)
            keep_in(t, grad_in(t, core, 0))

    def in_away(lo, hi):
        @pl.loop(lo, hi)
        def _(t):
            SD[t] = (SD[t].astype(F32) + grad_in(t, 1 - core, 1)).astype(BF16)
            swap(0, t).start()

    def out_away(lo, hi):
        @pl.loop(lo, hi)
        def _(t):
            SO[t] = grad_out(t, 1 - core).astype(BF16)
            swap(1, t).start()

    def in_here(lo, hi):
        @pl.loop(lo, hi)
        def _(t):
            second = grad_in(t, core, 1)
            swap(0, t).wait_recv()
            kept = [dqkv_ref[j, tile_rows(t), :] for j in range(3)] + [dup_ref[tile_rows(t), :]]
            first = jnp.concatenate(kept, axis=1).astype(F32)
            keep_in(t, first + second + RD[t].astype(F32))

    def out_here(lo, hi):
        @pl.loop(lo, hi)
        def _(t):
            own = grad_out(t, core)
            swap(1, t).wait_recv()
            cols = pl.ds(pl.multiple_of(t * TILE, TILE), TILE)
            total = (own + RO[t].astype(F32)).astype(BF16)
            dproj_ref[:, cols] = total[:HEAD]
            ddown_ref[:, cols] = total[HEAD:]

    def gain_send(stage, slots, me, tos):
        return [
            send(slots.at[me], slots.at[me], g_s.at[stage, i], g_r.at[stage, i], to)
            for i, to in enumerate(tos)
        ]

    def wait_all(cps):
        for cp in cps:
            cp.wait_recv()

    def owner_copy(dy):
        yy = (y + dy) % 4
        return copy(
            G.at[yy % 2, yy // 2, x, zrow, :], YR.at[y], z_s.at[dy - 1], z_r.at[dy - 1], dev(dy=dy)
        )

    def to_owner(k):
        @pl.when(y_lo == k)
        def _():
            owner_copy(2).start()

        @pl.when(y_lo != k)
        def _():
            owner_copy(1).start()
            owner_copy(3).start()

    own, other = y_hi, 1 - y_hi
    wait_all(y_in)
    ag_own(0, 0)
    wait_all(y_out)
    ag_own(1, 0)
    ag_fwd(0, 0)
    ag_end(0, 0)
    ag_own(0, 1)
    ag_fwd(1, 0)
    ag_own(2, 0)
    ag_fwd(0, 1)
    ag_end(1, 0)
    ag_fwd(2, 0)
    for cp in loads:
        cp.wait()
    ag_wait(0, 1, 1)
    ag_own(1, 1)
    ag_own(3, 0)
    ag_end(0, 1)
    e_in0 = partial_in(0)
    ag_fwd(1, 1)
    ag_end(2, 0)
    ag_fwd(3, 0)
    ag_wait(1, 1, 1)
    ag_own(2, 1)
    ag_end(1, 1)
    e_out0 = partial_out(0)
    ag_fwd(2, 1)
    ag_end(3, 0)
    ag_wait(2, 1, 1)
    ag_own(3, 1)
    wait_all((e_in0, e_out0))
    back0 = middle(0)
    normed_grad(0, own)
    ag_end(2, 1)
    e_in1 = partial_in(1)
    ag_fwd(3, 1)
    back0.wait_recv()
    normed_grad(0, other)
    ag_wait(3, 1, 1)
    ag_end(3, 1)
    rs_start(0, 1, own, 0)
    rs_start(0, 1, other, 1)
    e_out1 = partial_out(1)
    in_first()
    wait_all((e_in1, e_out1))
    back1 = middle(1)
    rs_mid(0, 1, own, 0)
    rs_mid(0, 1, other, 1)
    normed_grad(1, own)
    rs_start(1, 1, own, 0)
    rs_end(0, 1, own, 0)
    rs_start(0, 0, own, 0)
    rs_end(0, 1, other, 1)
    rs_start(0, 0, other, 1)
    back1.wait_recv()
    acts = [swap_act(0), swap_act(1)]
    normed_grad(1, other)
    rs_start(1, 1, other, 1)
    rs_mid(0, 0, own, 0)
    rs_mid(0, 0, other, 1)
    rs_mid(1, 1, own, 0)
    gsum = jnp.sum(GS[...], axis=0, keepdims=True)
    for j in range(HALF // HEAD):
        GC[core, j : j + 1, :] = gsum[:, j * HEAD : (j + 1) * HEAD]
    GC[core, 24:32, :] = GQ[...]
    g0 = gain_send(0, GC, core, [dev(dc=1)])
    in_away(0, 6)
    rs_end(0, 0, own, 0)
    rs_end(0, 0, other, 1)
    to_owner(0)
    rs_mid(1, 1, other, 1)
    wait_all(g0)
    GY[y] = GC[0] + GC[1]
    g1 = gain_send(1, GY, y, [dev(dy=d) for d in (1, 2, 3)])
    in_here(0, 6)
    rs_end(1, 1, own, 0)
    rs_start(1, 0, own, 0)
    wait_all(acts)
    out_away(0, 3)
    rs_end(1, 1, other, 1)
    rs_start(1, 0, other, 1)
    out_away(3, 6)
    rs_mid(1, 0, own, 0)
    wait_all(g1)
    GX[x, 0] = GY[0] + GY[1]
    GX[x, 1] = GY[2] + GY[3]
    g2 = gain_send(2, GX, x, [dev(dx=d) for d in (1, 2, 3)])
    rs_mid(1, 0, other, 1)
    out_here(0, 2)
    rs_end(1, 0, own, 0)
    rs_end(1, 0, other, 1)
    to_owner(1)
    YR[y] = G[y_lo, y_hi, x, zrow, :]
    wait_all(g2)
    GZ[z] = ((GX[0] + GX[1]) + GX[2]) + GX[3]
    g3 = gain_send(3, GZ, z, [dev(dz=d) for d in (1, 2, 3)])
    out_here(2, 6)
    wait_all(g3)
    gains = ((GZ[0] + GZ[1]) + GZ[2]) + GZ[3]
    for h in (0, 1):
        rows = slice(h * 24, (h + 1) * 24)
        gsum_ref[rows, :] = gains[h, 0:24, :] / gain_rows_ref[rows, :]
    qk_ref[...] = gains[0, 24:26, :] + gains[1, 24:26, :]
    for dy in (1, 2, 3):
        owner_copy(dy).wait_recv()
    inner = jnp.zeros((ROWS, 1), F32)
    for h in (0, 1):
        cols = slice(h * HALF, (h + 1) * HALF)
        c = (YR[2 * h].astype(F32) + YR[2 * h + 1].astype(F32)) * gain_ref[:, cols]
        inner += jnp.sum(c * tok_ref[:, cols].astype(F32), axis=1, keepdims=True)
    inner = inner / D
    for h in (0, 1):
        cols = slice(h * HALF, (h + 1) * HALF)
        c = (YR[2 * h].astype(F32) + YR[2 * h + 1].astype(F32)) * gain_ref[:, cols]
        own = tok_ref[:, cols].astype(F32)
        grad = og_ref[:, cols].astype(F32) + scale * c - own * (scale * scale * scale * inner)
        tg_ref[:, cols] = grad.astype(BF16)
    for cp in pending:
        cp.wait_send()
    for dy in (1, 2, 3):
        owner_copy(dy).wait_send()

    @pl.loop(0, tiles)
    def _(t):
        swap(0, t).wait_send()
        swap(1, t).wait_send()


def per_device(tokens, norm_gain, qkv_weight, up_weight, proj_weight, down_weight, query_gain, key_gain, out_grad):
    vm, hbm = pl.BlockSpec(memory_space=pltpu.VMEM), pl.BlockSpec(memory_space=pl.ANY)
    tiles = QUART // TILE
    quarter = HALF // 2
    dma = pltpu.SemaphoreType.DMA
    scratch = [
        pltpu.VMEM((ROWS, D), BF16),
        pltpu.VMEM((2, 2, 4, 64, HALF), BF16),
        pltpu.VMEM((2, 2, 4, 64, HALF), BF16),
        pltpu.VMEM((2, 2, 4, 64, HALF), BF16),
        pltpu.VMEM((HALF, W_IN), BF16),
        pltpu.VMEM((W_OUT, HALF), BF16),
        pltpu.VMEM((2, PATCHES, W_IN + W_OUT), BF16),
        pltpu.VMEM((2, PATCHES, W_IN + W_OUT), BF16),
        pltpu.VMEM((2, PATCHES, W_IN + W_OUT), F32),
        pltpu.VMEM((2, 2, PATCHES, W_IN), BF16),
        pltpu.VMEM((2, 2, PATCHES, W_OUT), BF16),
        pltpu.VMEM((2, 2, 4, ROWS, quarter), BF16),
        pltpu.VMEM((2, 2, 2, 4, ROWS, quarter), BF16),
        pltpu.VMEM((2, 2, 64, quarter), BF16),
        pltpu.VMEM((2, 2, 2, 64, quarter), BF16),
        pltpu.VMEM((2, 2, 2, ROWS, quarter), BF16),
        pltpu.VMEM((2, 2, 2, 2, ROWS, quarter), BF16),
        pltpu.VMEM((4, ROWS, HALF), BF16),
        pltpu.VMEM((tiles, TILE, W_IN), BF16),
        pltpu.VMEM((tiles, TILE, W_IN), BF16),
        pltpu.VMEM((tiles, W_OUT, TILE), BF16),
        pltpu.VMEM((tiles, W_OUT, TILE), BF16),
        pltpu.VMEM((8, HALF), F32),
        pltpu.VMEM((8, HEAD), F32),
        pltpu.VMEM((2, 32, HEAD), F32),
        pltpu.VMEM((4, 32, HEAD), F32),
        pltpu.VMEM((4, 2, 32, HEAD), F32),
        pltpu.VMEM((4, 2, 32, HEAD), F32),
        dma((6,)),
        dma((2, 3)),
        dma((2, 3)),
        dma((4, 2, 2, 2, 3)),
        dma((4, 2, 2, 2, 3)),
        dma((2, 4)),
        dma((2, 4)),
        dma((2, 2, 2, 2, 3)),
        dma((2, 2, 2, 2, 3)),
        dma((3,)),
        dma((3,)),
        dma((2, tiles)),
        dma((2, tiles)),
        dma((4, 3)),
        dma((4, 3)),
    ]
    token_grad, gain_grad, qk_grad, dqkv, dup, dproj, ddown = pl.pallas_call(
        kernel,
        name="block",
        out_shape=(
            jax.ShapeDtypeStruct((ROWS, D), BF16),
            jax.ShapeDtypeStruct((D // HEAD, HEAD), F32),
            jax.ShapeDtypeStruct((2, HEAD), F32),
            jax.ShapeDtypeStruct((3, QUART, HEAD), BF16),
            jax.ShapeDtypeStruct((QUART, UP), BF16),
            jax.ShapeDtypeStruct((HEAD, QUART), BF16),
            jax.ShapeDtypeStruct((UP, QUART), BF16),
        ),
        in_specs=[vm] * 6 + [hbm] * 4,
        out_specs=(vm,) * 7,
        scratch_shapes=scratch,
        compiler_params=pltpu.CompilerParams(
            collective_id=0, has_side_effects=True, vmem_limit_bytes=60 * 1024 * 1024
        ),
        cost_estimate=pl.CostEstimate(flops=21 * 10**9, bytes_accessed=20 * 10**6, transcendentals=0),
    )(
        tokens, out_grad, norm_gain.reshape(1, D), norm_gain.reshape(D // HEAD, HEAD),
        query_gain.reshape(1, HEAD), key_gain.reshape(1, HEAD),
        jnp.transpose(qkv_weight, (1, 0, 2)), up_weight, proj_weight, down_weight,
    )
    return finish(token_grad, gain_grad, qk_grad, dqkv, dup, dproj, ddown)


def widen(tg_ref, gain_ref, qk_ref, dqkv_ref, dup_ref, dproj_ref, ddown_ref, *outs):
    tg_out, gain_out, qk_out, dqkv_out, dup_out, dproj_out, ddown_out = outs

    @pl.when(pl.program_id(0) == 0)
    def _():
        tg_out[...] = tg_ref[...]
        gain_out[...] = gain_ref[...]
        qk_out[...] = qk_ref[...]

    for src, dst in ((dqkv_ref, dqkv_out), (dup_ref, dup_out), (dproj_ref, dproj_out), (ddown_ref, ddown_out)):
        dst[...] = src[...].astype(F32)


def finish(*arrays):
    steps = 6
    block = QUART // steps
    whole = [pl.BlockSpec(a.shape, lambda i: (0, 0)) for a in arrays[:3]]
    specs = whole + [
        pl.BlockSpec((3, block, HEAD), lambda i: (0, i, 0)),
        pl.BlockSpec((block, UP), lambda i: (i, 0)),
        pl.BlockSpec((HEAD, block), lambda i: (0, i)),
        pl.BlockSpec((UP, block), lambda i: (0, i)),
    ]
    shapes = [jax.ShapeDtypeStruct(a.shape, a.dtype) for a in arrays[:3]]
    shapes += [jax.ShapeDtypeStruct(a.shape, F32) for a in arrays[3:]]
    token_grad, gain_grad, qk_grad, dqkv, dup, dproj, ddown = pl.pallas_call(
        widen, name="widen", grid=(steps,), in_specs=specs, out_specs=specs, out_shape=shapes
    )(*arrays)
    return token_grad, gain_grad.reshape(D), qk_grad, jnp.transpose(dqkv, (1, 0, 2)), dup, dproj, ddown


def solution(mesh):
    rows = P(("dp", "mp"), None)
    placed = (rows, P(), P(None, None, "mp"), P(None, "mp"), P("mp", None), P("mp", None), P(), P(), rows)
    outs = (rows, P(), P(), P("dp", None, "mp"), P("dp", "mp"), P("mp", "dp"), P("mp", "dp"))
    return jax.shard_map(per_device, mesh=mesh, in_specs=placed, out_specs=outs, check_vma=False)
```

```python
import jax
import jax.numpy as jnp
from jax import lax
from jax.experimental import pallas as pl
from jax.experimental.pallas import tpu as pltpu
from jax.sharding import PartitionSpec as P

F32, BF16 = jnp.float32, jnp.bfloat16
MESH = pl.DeviceIdType.MESH

D = 6144
HALF = D // 2
QUART = D // 4
PATCHES = 256
HEAD = 128
UP = 384
W_IN = 3 * HEAD + UP
W_OUT = HEAD + UP
ROWS = 16
TILE = 256
WIDE = 512
PART = (slice(0, HALF // 2), slice(HALF // 2, HALF))
SUB = HALF // 4
EPS = 1e-06
GELU_A, GELU_B = 0.7978845608028654, 0.044715


def dot(left, right, dims):
    return lax.dot_general(left, right, (dims, ((), ())), preferred_element_type=F32)


def kernel(
    tok_ref, og_ref, gain_ref, gain_rows_ref, qg_ref, kg_ref, wqkv_ref, wup_ref, wproj_ref, wdown_ref,
    tg_ref, gsum_ref, qk_ref, dqkv_hbm, dup_hbm, dproj_hbm, ddown_hbm,
    nrm, N, C, G, win, wout, XS, XR, H, HG, ACT, FB1, MB1, FB2, MB2, FS, MS, YR,
    SD, RD, SO, RO, GS, GQ, GC, GY, GX, GZ,
    dqkv_ref, dup_ref, dproj_ref, ddown_ref, osem, wsem, y_s, y_r, ag_s, ag_f, ag_r, e_s, e_r, rs_s, rs_f, rs_r, z_s, z_r, d_s, d_r, g_s, g_r,
):
    dp, mp = lax.axis_index("dp"), lax.axis_index("mp")
    y_hi, core = dp // 2, dp % 2
    y_lo, x, z = mp // 16, (mp // 4) % 4, mp % 4
    y = y_hi * 2 + y_lo

    def dev(dx=0, dy=0, dz=0, dc=0):
        xx, yy, zz, cc = (x + dx) % 4, (y + dy) % 4, (z + dz) % 4, (core + dc) % 2
        return ((yy // 2) * 2 + cc, (yy % 2) * 16 + xx * 4 + zz)

    def copy(src, dst, send, recv, to):
        return pltpu.make_async_remote_copy(
            src_ref=src, dst_ref=dst, send_sem=send, recv_sem=recv, device_id=to, device_id_type=MESH
        )

    pending = []

    def begin(*args):
        cp = copy(*args)
        cp.start()
        return cp

    def take(sem, view):
        pltpu.make_async_copy(view, view, sem).wait()

    def blocks(count):
        rows, cols = {2: (32, 1), 6: (32, 1), 24: (64, 2)}.get(count, (64, 1))
        groups = count * ROWS // (rows * cols)
        if count == 48:
            return N.at[0, :, 0:3]
        return N.at[0, 0, 0:groups, 0:rows, 0 : cols * (HALF // 2)]

    def drain(upto):
        for cp in pending[:upto]:
            cp.wait_send()
        del pending[:upto]

    def send(*args):
        cp = copy(*args)
        cp.start()
        pending.append(cp)
        return cp

    half = pl.ds(pl.multiple_of(y_hi * HALF, HALF), HALF)
    loads = [
        pltpu.make_async_copy(wqkv_ref.at[j, half], win.at[:, pl.ds(j * HEAD, HEAD)], wsem.at[j])
        for j in range(3)
    ]
    loads.append(pltpu.make_async_copy(wup_ref.at[half], win.at[:, pl.ds(3 * HEAD, UP)], wsem.at[3]))
    loads.append(pltpu.make_async_copy(wproj_ref.at[:, half], wout.at[pl.ds(0, HEAD)], wsem.at[4]))
    loads.append(pltpu.make_async_copy(wdown_ref.at[:, half], wout.at[pl.ds(HEAD, UP)], wsem.at[5]))
    for cp in loads:
        cp.start()

    barrier = pltpu.get_barrier_semaphore()
    peers = [dev(dy=d) for d in (1, 2, 3)] + [dev(dx=d) for d in (1, 2, 3)]
    peers += [dev(dz=d) for d in (1, 2, 3)] + [dev(dc=1)]
    for peer in peers:
        pl.semaphore_signal(barrier, inc=1, device_id=peer, device_id_type=MESH)

    zrow = pl.ds(pl.multiple_of(z * ROWS, ROWS), ROWS)

    tok = tok_ref[...].astype(F32)
    scale = lax.rsqrt(jnp.mean(tok * tok, axis=1, keepdims=True) + EPS)
    nrm[...] = (tok * scale * gain_ref[...]).astype(BF16)
    N[y_lo, y_hi, x, zrow, :] = nrm[:, half]
    C[y_lo, y_hi, x, zrow, :] = og_ref[:, half]
    pl.semaphore_wait(barrier, len(peers))

    def along_y(a, src, dst):
        row = {}
        for dy in (1, 2, 3):
            there = ((y + dy) % 4) // 2
            cols = pl.ds(pl.multiple_of(there * HALF, HALF), HALF)
            row[dy] = copy(src.at[:, cols], dst.at[y_lo, y_hi, x, zrow, :],
                           y_s.at[a, dy - 1], y_r.at[a, dy - 1], dev(dy=dy))
        return row

    y_copies = [along_y(0, nrm, N), along_y(1, og_ref, C)]

    def y_start(a, k):
        @pl.when(y_lo == k)
        def _():
            for dy in (1, 3, 2):
                y_copies[a][dy].start()

    def y_wait(a, k):
        @pl.when(y_lo == k)
        def _():
            y_copies[a][2].wait_recv()

        @pl.when(y_lo != k)
        def _():
            y_copies[a][1].wait_recv()
            y_copies[a][3].wait_recv()

    y_start(0, 0)
    GS[...] = jnp.zeros_like(GS)
    GQ[...] = jnp.zeros_like(GQ)

    def zr(i):
        return pl.ds(pl.multiple_of(((z + i) % 4) * ROWS, ROWS), ROWS)

    def ag_first(ref, k, p, off, yh):
        if p == 0:
            return ref.at[k, yh, (x + off) % 4, zrow, PART[0]]
        return ref.at[k, yh, x, zr(off), PART[1]]

    def ag_second(ref, k, p, off, yh):
        if p == 0:
            return ref.at[k, yh, :, zr(off), PART[0]]
        return ref.at[k, yh, (x + off) % 4, :, PART[1]]

    def ag_dev(p, phase, step):
        return dev(dx=step) if p == phase else dev(dz=step)

    units = [(N, 0), (C, 0), (N, 1), (C, 1)]
    ag = {}

    def ag_own(u, phase):
        ref, k = units[u]
        where = (ag_first, ag_second)[phase]
        for first in (0, 1):
            for p in (0, 1):
                for d, step in enumerate((1, -1)):
                    block = where(ref, k, p, 0, d if first == 0 else 1 - d)
                    recv = ag_f.at[u, phase, p, d] if first == 0 else ag_r.at[u, phase, 0]
                    cp = begin(block, block, ag_s.at[u, phase], recv, ag_dev(p, phase, step))
                    if first == 0:
                        ag[u, phase, p, d] = cp

    def ag_fwd(u, phase):
        ref, k = units[u]
        where = (ag_first, ag_second)[phase]
        for p in (0, 1):
            for d, step in enumerate((1, -1)):
                ag[u, phase, p, d].wait_recv()
                block = where(ref, k, p, -step, d)
                begin(block, block, ag_s.at[u, phase], ag_r.at[u, phase, 1], ag_dev(p, phase, step))

    def ag_wait(u, phase, i):
        take(ag_r.at[u, phase, i - 1], blocks((4, 16)[phase]))

    def ag_end(u, phase):
        if phase == 0:
            ag_wait(u, phase, 1)
        ag_wait(u, phase, 2)

    def ag_sent():
        for u in range(4):
            for phase in (0, 1):
                take(ag_s.at[u, phase], blocks((12, 48)[phase]))

    partner = dev(dy=2)

    def rows_of(ref, k, yh):
        return ref[k, yh].reshape(PATCHES, HALF)

    def partial_in(k):
        other = 1 - y_hi

        @pl.loop(0, W_IN // TILE)
        def _(j):
            cols = pl.ds(pl.multiple_of(j * TILE, TILE), TILE)
            XS[k, :, cols] = dot(rows_of(N, k, other), win[:, cols], ((1,), (0,))).astype(BF16)

        cp = send(XS.at[k, :, pl.ds(0, W_IN)], XR.at[k, :, pl.ds(0, W_IN)], e_s.at[k, 0], e_r.at[k, 0], partner)

        @pl.loop(0, W_IN // TILE)
        def _(j):
            cols = pl.ds(pl.multiple_of(j * TILE, TILE), TILE)
            H[k, :, cols] = dot(rows_of(N, k, y_hi), win[:, cols], ((1,), (0,)))

        return cp

    def partial_out(k):
        other = 1 - y_hi

        @pl.loop(0, W_OUT // TILE)
        def _(j):
            rows = pl.ds(pl.multiple_of(j * TILE, TILE), TILE)
            cols = pl.ds(pl.multiple_of(W_IN + j * TILE, TILE), TILE)
            XS[k, :, cols] = dot(rows_of(C, k, other), wout[rows, :], ((1,), (1,))).astype(BF16)

        cp = send(XS.at[k, :, pl.ds(W_IN, W_OUT)], XR.at[k, :, pl.ds(W_IN, W_OUT)],
                  e_s.at[k, 1], e_r.at[k, 1], partner)

        @pl.loop(0, W_OUT // TILE)
        def _(j):
            rows = pl.ds(pl.multiple_of(j * TILE, TILE), TILE)
            cols = pl.ds(pl.multiple_of(W_IN + j * TILE, TILE), TILE)
            H[k, :, cols] = dot(rows_of(C, k, y_hi), wout[rows, :], ((1,), (1,)))

        return cp

    def summed(k, start, width, rows=slice(None)):
        cols = pl.ds(start, width)
        return H[k, rows, cols] + XR[k, rows, cols].astype(F32)

    def head_norm(h, g):
        factor = lax.rsqrt(jnp.mean(h * h, axis=1, keepdims=True) + EPS)
        return factor, (h * factor * g).astype(BF16)

    def head_norm_back(h, factor, g, dy):
        hf = h * factor
        dyg = dy * g
        dh = factor * (dyg - hf * jnp.mean(hf * dyg, axis=1, keepdims=True))
        return dh, jnp.sum(dy * hf, axis=0, keepdims=True)

    def middle(k):
        hq, hk = summed(k, 0, HEAD), summed(k, HEAD, HEAD)
        v = summed(k, 2 * HEAD, HEAD).astype(BF16)
        da = summed(k, W_IN, HEAD).astype(BF16)
        qg, kg = qg_ref[...], kg_ref[...]
        fq, qn = head_norm(hq, qg)
        fk, kn = head_norm(hk, kg)
        w = jnp.exp(dot(qn, kn, ((1,), (1,))) * HEAD**-0.5)
        probs = w / jnp.sum(w, axis=1, keepdims=True)
        probs_b = probs.astype(BF16)
        ACT[k, y_hi, :, 0:HEAD] = dot(probs_b, v, ((1,), (0,))).astype(BF16)
        dpr = dot(da, v, ((1,), (1,))).astype(BF16).astype(F32)
        HG[k, y_hi, :, 2 * HEAD : 3 * HEAD] = dot(probs_b, da, ((0,), (0,))).astype(BF16)
        ds = probs * (dpr - jnp.sum(probs * dpr, axis=1, keepdims=True))
        ds = (ds * HEAD**-0.5).astype(BF16)
        dqn = dot(ds, kn, ((1,), (0,))).astype(BF16).astype(F32)
        dkn = dot(ds, qn, ((0,), (0,))).astype(BF16).astype(F32)
        dhq, dqg = head_norm_back(hq, fq, qg, dqn)
        dhk, dkg = head_norm_back(hk, fk, kg, dkn)
        HG[k, y_hi, :, 0:HEAD] = dhq.astype(BF16)
        HG[k, y_hi, :, HEAD : 2 * HEAD] = dhk.astype(BF16)
        GQ[0:1, :] += dqg
        GQ[1:2, :] += dkg

        @pl.loop(0, 4)
        def _(i):
            rows = pl.ds(pl.multiple_of(i * 64, 64), 64)
            u = summed(k, 3 * HEAD, UP, rows)
            dact = summed(k, W_IN + HEAD, UP, rows).astype(BF16).astype(F32)
            t = jnp.tanh(GELU_A * (u + GELU_B * (u * u * u)))
            ACT[k, y_hi, rows, HEAD:] = (0.5 * u * (1.0 + t)).astype(BF16)
            slope = 0.5 * (1.0 + t) + 0.5 * u * (1.0 - t * t) * (GELU_A * (1.0 + 3.0 * GELU_B * (u * u)))
            HG[k, y_hi, rows, 3 * HEAD :] = (dact * slope).astype(BF16)

        return send(HG.at[k, y_hi], HG.at[k, y_hi], e_s.at[k, 2], e_r.at[k, 2], partner)

    def swap_act(k):
        return send(ACT.at[k, y_hi], ACT.at[k, y_hi], e_s.at[k, 3], e_r.at[k, 3], partner)

    def normed_grad(k, yh):
        @pl.loop(0, HALF // WIDE)
        def _(j):
            cols = pl.ds(pl.multiple_of(j * WIDE, WIDE), WIDE)
            ng = dot(HG[k, yh], win[cols, :], ((1,), (1,)))
            G[k, yh, :, :, cols] = ng.astype(BF16).reshape(4, 64, WIDE)
            term = ng * N[k, yh, :, :, cols].reshape(PATCHES, WIDE).astype(F32)
            GS[:, cols] += jnp.sum(term.reshape(PATCHES // 8, 8, WIDE), axis=0)

    def rs_bufs(k, phase, p):
        if phase == 1:
            return (FB1, FB2)[p].at[k], (MB1, MB2)[p].at[k]
        return FS.at[p, k], MS.at[p, k]

    def rs_cut(phase, p, view, s):
        cols = pl.ds(s * SUB, SUB)
        return view.at[:, :, cols] if phase == 1 and p == 0 else view.at[:, cols]

    def rs_steps(k, phase, yh):
        where = (ag_first, ag_second)[phase]
        for p in (0, 1):
            fr, mr = rs_bufs(k, phase, p)
            for s, step in enumerate((1, -1)):
                block = lambda off: rs_cut(phase, p, where(G, k, p, off, yh), s)
                far = rs_cut(phase, p, fr.at[yh], s)
                near = [rs_cut(phase, p, mr.at[i, yh], s) for i in (0, 1)]
                yield p, step, block, far, near

    def rs_far(k, phase, yh):
        for p, step, block, far, _ in rs_steps(k, phase, yh):
            begin(block(2), far, rs_s.at[k, phase, yh], rs_f.at[k, phase, yh], ag_dev(p, phase, step))

    def rs_near(k, phase, yh):
        for p, step, block, _, near in rs_steps(k, phase, yh):
            begin(block(-step), near[1], rs_s.at[k, phase, yh], rs_r.at[k, phase, yh], ag_dev(p, phase, -step))

    def rs_start(k, phase, yh):
        rs_far(k, phase, yh)
        rs_near(k, phase, yh)

    def rs_mid(k, phase, yh):
        take(rs_f.at[k, phase, yh], blocks((2, 8)[phase]))
        for p, step, block, far, near in rs_steps(k, phase, yh):
            mine = block(step)
            mine[...] = (mine[...].astype(F32) + far[...].astype(F32)).astype(BF16)
            begin(mine, near[0], rs_s.at[k, phase, yh], rs_r.at[k, phase, yh], ag_dev(p, phase, step))

    def rs_end(k, phase, yh):
        take(rs_r.at[k, phase, yh], blocks((4, 16)[phase]))
        where = (ag_first, ag_second)[phase]
        for p in (0, 1):
            _, mr = rs_bufs(k, phase, p)
            block = where(G, k, p, 0, yh)
            total = block[...].astype(F32) + mr[0, yh].astype(F32) + mr[1, yh].astype(F32)
            block[...] = total.astype(BF16)

    def rs_sent():
        for k in (0, 1):
            for phase in (0, 1):
                for yh in (0, 1):
                    take(rs_s.at[k, phase, yh], blocks((6, 24)[phase]))

    def feature_tile(t, whose):
        return pl.ds(pl.multiple_of(whose * QUART + t * TILE, TILE), TILE)

    def grad_in(t, whose, k):
        left = N[k, :, :, :, feature_tile(t, whose)].reshape(2 * PATCHES, TILE)
        return dot(left, HG[k].reshape(2 * PATCHES, W_IN), ((0,), (0,)))

    def grad_out(t, whose, yh):
        right = C[:, yh, :, :, feature_tile(t, whose)].reshape(2 * PATCHES, TILE)
        return dot(ACT[:, yh].reshape(2 * PATCHES, W_OUT), right, ((0,), (0,)))

    def swap(kind, t):
        src, dst = ((SD, RD), (SO, RO))[kind]
        return copy(src.at[t], dst.at[t], d_s.at[kind], d_r.at[kind, t], dev(dc=1))

    tiles = QUART // TILE

    def tile_rows(t):
        return pl.ds(pl.multiple_of(t * TILE, TILE), TILE)

    def keep_in(t, total):
        for j in range(3):
            dqkv_ref[j, tile_rows(t), :] = total[:, j * HEAD : (j + 1) * HEAD].astype(BF16)
        dup_ref[tile_rows(t), :] = total[:, 3 * HEAD :].astype(BF16)

    def in_first(lo, hi):
        @pl.loop(lo, hi)
        def _(t):
            SD[t] = grad_in(t, 1 - core, 0).astype(BF16)
            keep_in(t, grad_in(t, core, 0))

    def keep_out(t, total):
        dproj_ref[:, tile_rows(t)] = total[:HEAD].astype(BF16)
        ddown_ref[:, tile_rows(t)] = total[HEAD:].astype(BF16)

    def out_first():
        @pl.loop(0, tiles)
        def _(t):
            SO[t] = grad_out(t, 1 - core, y_hi).astype(BF16)
            keep_out(t, grad_out(t, core, y_hi))

    def in_away(lo, hi):
        @pl.loop(lo, hi)
        def _(t):
            SD[t] = (SD[t].astype(F32) + grad_in(t, 1 - core, 1)).astype(BF16)
            swap(0, t).start()

    def out_away(lo, hi):
        @pl.loop(lo, hi)
        def _(t):
            SO[t] = (SO[t].astype(F32) + grad_out(t, 1 - core, 1 - y_hi)).astype(BF16)
            swap(1, t).start()

    def in_here(lo, hi):
        @pl.loop(lo, hi)
        def _(t):
            second = grad_in(t, core, 1)
            swap(0, t).wait_recv()
            kept = [dqkv_ref[j, tile_rows(t), :] for j in range(3)] + [dup_ref[tile_rows(t), :]]
            first = jnp.concatenate(kept, axis=1).astype(F32)
            keep_in(t, first + second + RD[t].astype(F32))

    def out_here(lo, hi):
        @pl.loop(lo, hi)
        def _(t):
            second = grad_out(t, core, 1 - y_hi)
            swap(1, t).wait_recv()
            kept = [dproj_ref[:, tile_rows(t)], ddown_ref[:, tile_rows(t)]]
            first = jnp.concatenate(kept, axis=0).astype(F32)
            keep_out(t, first + second + RO[t].astype(F32))

    def gain_send(stage, slots, me, tos):
        for to in tos:
            begin(slots.at[me], slots.at[me], g_s.at[stage], g_r.at[stage], to)

    gain_slots = [GC.at[0:1], GY.at[0:3], GX.at[0:3], GZ.at[0:3]]

    def gain_wait(stage):
        take(g_r.at[stage], gain_slots[stage])

    def gain_sent():
        for stage in range(4):
            take(g_s.at[stage], gain_slots[stage])

    def wait_all(cps):
        for cp in cps:
            cp.wait_recv()

    def owner_copy(dy):
        yy = (y + dy) % 4
        return copy(
            G.at[yy % 2, yy // 2, x, zrow, :], YR.at[y], z_s.at[dy - 1], z_r.at[dy - 1], dev(dy=dy)
        )

    def to_owner(k):
        @pl.when(y_lo == k)
        def _():
            owner_copy(2).start()

        @pl.when(y_lo != k)
        def _():
            owner_copy(1).start()
            owner_copy(3).start()

    results = ((dqkv_ref, dqkv_hbm), (dup_ref, dup_hbm), (dproj_ref, dproj_hbm), (ddown_ref, ddown_hbm))
    stores = [pltpu.make_async_copy(src, dst, osem.at[i]) for i, (src, dst) in enumerate(results)]

    own, other = y_hi, 1 - y_hi
    y_wait(0, 0)
    y_start(1, 0)
    ag_own(0, 0)
    y_wait(1, 0)
    ag_own(1, 0)
    y_start(0, 1)
    y_start(1, 1)
    ag_fwd(0, 0)
    ag_end(0, 0)
    ag_own(0, 1)
    ag_fwd(1, 0)
    y_wait(0, 1)
    ag_own(2, 0)
    ag_fwd(0, 1)
    ag_end(1, 0)
    ag_fwd(2, 0)
    for cp in loads:
        cp.wait()
    ag_wait(0, 1, 1)
    ag_own(1, 1)
    y_wait(1, 1)
    ag_own(3, 0)
    ag_end(0, 1)
    e_in0 = partial_in(0)
    ag_fwd(1, 1)
    ag_end(2, 0)
    ag_fwd(3, 0)
    ag_wait(1, 1, 1)
    ag_own(2, 1)
    ag_end(1, 1)
    e_out0 = partial_out(0)
    ag_fwd(2, 1)
    ag_end(3, 0)
    ag_wait(2, 1, 1)
    ag_own(3, 1)
    wait_all((e_in0, e_out0))
    back0 = middle(0)
    normed_grad(0, own)
    ag_end(2, 1)
    e_in1 = partial_in(1)
    ag_fwd(3, 1)
    back0.wait_recv()
    normed_grad(0, other)
    ag_wait(3, 1, 1)
    in_first(0, 3)
    ag_end(3, 1)
    rs_far(0, 1, own)
    rs_far(0, 1, other)
    e_out1 = partial_out(1)
    rs_near(0, 1, own)
    rs_near(0, 1, other)
    in_first(3, 6)
    rs_mid(0, 1, own)
    wait_all((e_in1, e_out1))
    back1 = middle(1)
    rs_mid(0, 1, other)
    normed_grad(1, own)
    rs_start(1, 1, own)
    rs_end(0, 1, own)
    rs_start(0, 0, own)
    rs_end(0, 1, other)
    rs_start(0, 0, other)
    out_first()
    back1.wait_recv()
    normed_grad(1, other)
    rs_start(1, 1, other)
    acts = [swap_act(0), swap_act(1)]
    rs_mid(0, 0, own)
    rs_mid(0, 0, other)
    rs_mid(1, 1, own)
    gsum = jnp.sum(GS[...], axis=0, keepdims=True)
    for j in range(HALF // HEAD):
        GC[core, j : j + 1, :] = gsum[:, j * HEAD : (j + 1) * HEAD]
    GC[core, 24:32, :] = GQ[...]
    gain_send(0, GC, core, [dev(dc=1)])
    in_away(0, 6)
    rs_mid(1, 1, other)
    rs_end(0, 0, own)
    rs_end(0, 0, other)
    to_owner(0)
    gain_wait(0)
    GY[y] = GC[0] + GC[1]
    gain_send(1, GY, y, [dev(dy=d) for d in (1, 2, 3)])
    rs_end(1, 1, own)
    rs_start(1, 0, own)
    in_here(0, 4)
    rs_end(1, 1, other)
    rs_start(1, 0, other)
    in_here(4, 6)
    for cp in stores[:2]:
        cp.start()
    rs_mid(1, 0, own)
    rs_mid(1, 0, other)
    gain_wait(1)
    GX[x, 0] = GY[0] + GY[1]
    GX[x, 1] = GY[2] + GY[3]
    gain_send(2, GX, x, [dev(dx=d) for d in (1, 2, 3)])
    wait_all(acts)
    out_away(0, 6)
    rs_end(1, 0, own)
    rs_end(1, 0, other)
    to_owner(1)
    YR[y] = G[y_lo, y_hi, x, zrow, :]
    gain_wait(2)
    GZ[z] = ((GX[0] + GX[1]) + GX[2]) + GX[3]
    gain_send(3, GZ, z, [dev(dz=d) for d in (1, 2, 3)])
    out_here(0, 6)
    for cp in stores[2:]:
        cp.start()
    ag_sent()
    rs_sent()
    gain_wait(3)
    gains = ((GZ[0] + GZ[1]) + GZ[2]) + GZ[3]
    for h in (0, 1):
        rows = slice(h * 24, (h + 1) * 24)
        gsum_ref[rows, :] = gains[h, 0:24, :] / gain_rows_ref[rows, :]
    qk_ref[...] = gains[0, 24:26, :] + gains[1, 24:26, :]
    for dy in (1, 2, 3):
        owner_copy(dy).wait_recv()
    inner = jnp.zeros((ROWS, 1), F32)
    for h in (0, 1):
        cols = slice(h * HALF, (h + 1) * HALF)
        c = (YR[2 * h].astype(F32) + YR[2 * h + 1].astype(F32)) * gain_ref[:, cols]
        inner += jnp.sum(c * tok_ref[:, cols].astype(F32), axis=1, keepdims=True)
    inner = inner / D
    for h in (0, 1):
        cols = slice(h * HALF, (h + 1) * HALF)
        c = (YR[2 * h].astype(F32) + YR[2 * h + 1].astype(F32)) * gain_ref[:, cols]
        own = tok_ref[:, cols].astype(F32)
        grad = og_ref[:, cols].astype(F32) + scale * c - own * (scale * scale * scale * inner)
        tg_ref[:, cols] = grad.astype(BF16)
    gain_sent()
    drain(len(pending))
    for cp in stores:
        cp.wait()
    for row in y_copies:
        for dy in (1, 2, 3):
            row[dy].wait_send()
    for dy in (1, 2, 3):
        owner_copy(dy).wait_send()
    take(d_s.at[0], SD)
    take(d_s.at[1], SO)


def per_device(tokens, norm_gain, qkv_weight, up_weight, proj_weight, down_weight, query_gain, key_gain, out_grad):
    vm, hbm = pl.BlockSpec(memory_space=pltpu.VMEM), pl.BlockSpec(memory_space=pl.ANY)
    tiles = QUART // TILE
    quarter = HALF // 2
    dma = pltpu.SemaphoreType.DMA
    scratch = [
        pltpu.VMEM((ROWS, D), BF16),
        pltpu.VMEM((2, 2, 4, 64, HALF), BF16),
        pltpu.VMEM((2, 2, 4, 64, HALF), BF16),
        pltpu.VMEM((2, 2, 4, 64, HALF), BF16),
        pltpu.VMEM((HALF, W_IN), BF16),
        pltpu.VMEM((W_OUT, HALF), BF16),
        pltpu.VMEM((2, PATCHES, W_IN + W_OUT), BF16),
        pltpu.VMEM((2, PATCHES, W_IN + W_OUT), BF16),
        pltpu.VMEM((2, PATCHES, W_IN + W_OUT), F32),
        pltpu.VMEM((2, 2, PATCHES, W_IN), BF16),
        pltpu.VMEM((2, 2, PATCHES, W_OUT), BF16),
        pltpu.VMEM((2, 2, 4, ROWS, quarter), BF16),
        pltpu.VMEM((2, 2, 2, 4, ROWS, quarter), BF16),
        pltpu.VMEM((2, 2, 64, quarter), BF16),
        pltpu.VMEM((2, 2, 2, 64, quarter), BF16),
        pltpu.VMEM((2, 2, 2, ROWS, quarter), BF16),
        pltpu.VMEM((2, 2, 2, 2, ROWS, quarter), BF16),
        pltpu.VMEM((4, ROWS, HALF), BF16),
        pltpu.VMEM((tiles, TILE, W_IN), BF16),
        pltpu.VMEM((tiles, TILE, W_IN), BF16),
        pltpu.VMEM((tiles, W_OUT, TILE), BF16),
        pltpu.VMEM((tiles, W_OUT, TILE), BF16),
        pltpu.VMEM((8, HALF), F32),
        pltpu.VMEM((8, HEAD), F32),
        pltpu.VMEM((2, 32, HEAD), F32),
        pltpu.VMEM((4, 32, HEAD), F32),
        pltpu.VMEM((4, 2, 32, HEAD), F32),
        pltpu.VMEM((4, 2, 32, HEAD), F32),
        pltpu.VMEM((3, QUART, HEAD), BF16),
        pltpu.VMEM((QUART, UP), BF16),
        pltpu.VMEM((HEAD, QUART), BF16),
        pltpu.VMEM((UP, QUART), BF16),
        dma((4,)),
        dma((6,)),
        dma((2, 3)),
        dma((2, 3)),
        dma((4, 2)),
        dma((4, 2, 2, 2)),
        dma((4, 2, 2)),
        dma((2, 4)),
        dma((2, 4)),
        dma((2, 2, 2)),
        dma((2, 2, 2)),
        dma((2, 2, 2)),
        dma((3,)),
        dma((3,)),
        dma((2,)),
        dma((2, tiles)),
        dma((4,)),
        dma((4,)),
    ]
    token_grad, gain_grad, qk_grad, dqkv, dup, dproj, ddown = pl.pallas_call(
        kernel,
        name="block",
        out_shape=(
            jax.ShapeDtypeStruct((ROWS, D), BF16),
            jax.ShapeDtypeStruct((D // HEAD, HEAD), F32),
            jax.ShapeDtypeStruct((2, HEAD), F32),
            jax.ShapeDtypeStruct((3, QUART, HEAD), BF16),
            jax.ShapeDtypeStruct((QUART, UP), BF16),
            jax.ShapeDtypeStruct((HEAD, QUART), BF16),
            jax.ShapeDtypeStruct((UP, QUART), BF16),
        ),
        in_specs=[vm] * 6 + [hbm] * 4,
        out_specs=(vm,) * 3 + (hbm,) * 4,
        scratch_shapes=scratch,
        compiler_params=pltpu.CompilerParams(
            collective_id=0, has_side_effects=True, vmem_limit_bytes=60 * 1024 * 1024
        ),
        cost_estimate=pl.CostEstimate(flops=21 * 10**9, bytes_accessed=20 * 10**6, transcendentals=0),
    )(
        tokens, out_grad, norm_gain.reshape(1, D), norm_gain.reshape(D // HEAD, HEAD),
        query_gain.reshape(1, HEAD), key_gain.reshape(1, HEAD),
        jnp.transpose(qkv_weight, (1, 0, 2)), up_weight, proj_weight, down_weight,
    )
    return finish(token_grad, gain_grad, qk_grad, dqkv, dup, dproj, ddown)


def widen(tg_ref, gain_ref, qk_ref, dqkv_ref, dup_ref, dproj_ref, ddown_ref, *outs):
    tg_out, gain_out, qk_out, dqkv_out, dup_out, dproj_out, ddown_out = outs

    @pl.when(pl.program_id(0) == 0)
    def _():
        tg_out[...] = tg_ref[...]
        gain_out[...] = gain_ref[...]
        qk_out[...] = qk_ref[...]

    for src, dst in ((dqkv_ref, dqkv_out), (dup_ref, dup_out), (dproj_ref, dproj_out), (ddown_ref, ddown_out)):
        dst[...] = src[...].astype(F32)


def finish(*arrays):
    steps = 2
    block = QUART // steps
    whole = [pl.BlockSpec(a.shape, lambda i: (0, 0)) for a in arrays[:3]]
    specs = whole + [
        pl.BlockSpec((3, block, HEAD), lambda i: (0, i, 0)),
        pl.BlockSpec((block, UP), lambda i: (i, 0)),
        pl.BlockSpec((HEAD, block), lambda i: (0, i)),
        pl.BlockSpec((UP, block), lambda i: (0, i)),
    ]
    shapes = [jax.ShapeDtypeStruct(a.shape, a.dtype) for a in arrays[:3]]
    shapes += [jax.ShapeDtypeStruct(a.shape, F32) for a in arrays[3:]]
    token_grad, gain_grad, qk_grad, dqkv, dup, dproj, ddown = pl.pallas_call(
        widen, name="widen", grid=(steps,), in_specs=specs, out_specs=specs, out_shape=shapes
    )(*arrays)
    return token_grad, gain_grad.reshape(D), qk_grad, jnp.transpose(dqkv, (1, 0, 2)), dup, dproj, ddown


def solution(mesh):
    rows = P(("dp", "mp"), None)
    placed = (rows, P(), P(None, None, "mp"), P(None, "mp"), P("mp", None), P("mp", None), P(), P(), rows)
    outs = (rows, P(), P(), P("dp", None, "mp"), P("dp", "mp"), P("mp", "dp"), P("mp", "dp"))
    return jax.shard_map(per_device, mesh=mesh, in_specs=placed, out_specs=outs, check_vma=False)
```

```python
import jax
import jax.numpy as jnp
from jax import lax
from jax.experimental import pallas as pl
from jax.experimental.pallas import tpu as pltpu
from jax.sharding import PartitionSpec as P

F32, BF16 = jnp.float32, jnp.bfloat16
MESH = pl.DeviceIdType.MESH

D = 6144
HALF = D // 2
QUART = D // 4
PATCHES = 256
HEAD = 128
UP = 384
W_IN = 3 * HEAD + UP
W_OUT = HEAD + UP
ROWS = 16
TILE = 256
WIDE = 512
PART = (slice(0, HALF // 2), slice(HALF // 2, HALF))
SUB = HALF // 4
EPS = 1e-06
GELU_A, GELU_B = 0.7978845608028654, 0.044715


def dot(left, right, dims):
    return lax.dot_general(left, right, (dims, ((), ())), preferred_element_type=F32)


def kernel(
    tok_ref, og_ref, gain_ref, gain_rows_ref, qg_ref, kg_ref, wqkv_ref, wup_ref, wproj_ref, wdown_ref,
    tg_ref, gsum_ref, qk_ref, dqkv_hbm, dup_hbm, dproj_hbm, ddown_hbm,
    nrm, N, C, G, win, wout, XS, XR, H, HG, ACT, FB1, MB1, FB2, MB2, FS, MS, YR,
    SD, RD, SO, RO, GS, GQ, GC, GY, GX, GZ,
    dqkv_ref, dup_ref, dproj_ref, ddown_ref, osem, wsem, y_s, y_r, ag_s, ag_f, ag_r, e_s, e_r, rs_s, rs_f, rs_r, z_s, z_r, d_s, d_r, g_s, g_r,
):
    dp, mp = lax.axis_index("dp"), lax.axis_index("mp")
    y_hi, core = dp // 2, dp % 2
    y_lo, x, z = mp // 16, (mp // 4) % 4, mp % 4
    y = y_hi * 2 + y_lo

    def dev(dx=0, dy=0, dz=0, dc=0):
        xx, yy, zz, cc = (x + dx) % 4, (y + dy) % 4, (z + dz) % 4, (core + dc) % 2
        return ((yy // 2) * 2 + cc, (yy % 2) * 16 + xx * 4 + zz)

    def copy(src, dst, send, recv, to):
        return pltpu.make_async_remote_copy(
            src_ref=src, dst_ref=dst, send_sem=send, recv_sem=recv, device_id=to, device_id_type=MESH
        )

    pending = []

    def begin(*args):
        cp = copy(*args)
        cp.start()
        return cp

    def take(sem, view):
        pltpu.make_async_copy(view, view, sem).wait()

    def blocks(count):
        rows, cols = {1: (16, 1), 2: (32, 1), 6: (32, 1), 24: (64, 2)}.get(count, (64, 1))
        groups = count * ROWS // (rows * cols)
        if count == 48:
            return N.at[0, :, 0:3]
        return N.at[0, 0, 0:groups, 0:rows, 0 : cols * (HALF // 2)]

    def drain(upto):
        for cp in pending[:upto]:
            cp.wait_send()
        del pending[:upto]

    def send(*args):
        cp = copy(*args)
        cp.start()
        pending.append(cp)
        return cp

    half = pl.ds(pl.multiple_of(y_hi * HALF, HALF), HALF)
    loads = [
        pltpu.make_async_copy(wqkv_ref.at[j, half], win.at[:, pl.ds(j * HEAD, HEAD)], wsem.at[j])
        for j in range(3)
    ]
    loads.append(pltpu.make_async_copy(wup_ref.at[half], win.at[:, pl.ds(3 * HEAD, UP)], wsem.at[3]))
    loads.append(pltpu.make_async_copy(wproj_ref.at[:, half], wout.at[pl.ds(0, HEAD)], wsem.at[4]))
    loads.append(pltpu.make_async_copy(wdown_ref.at[:, half], wout.at[pl.ds(HEAD, UP)], wsem.at[5]))
    for cp in loads:
        cp.start()

    barrier = pltpu.get_barrier_semaphore()
    peers = [dev(dy=d) for d in (1, 2, 3)] + [dev(dx=d) for d in (1, 2, 3)]
    peers += [dev(dz=d) for d in (1, 2, 3)] + [dev(dc=1)]
    for peer in peers:
        pl.semaphore_signal(barrier, inc=1, device_id=peer, device_id_type=MESH)

    zrow = pl.ds(pl.multiple_of(z * ROWS, ROWS), ROWS)

    tok = tok_ref[...].astype(F32)
    scale = lax.rsqrt(jnp.mean(tok * tok, axis=1, keepdims=True) + EPS)
    nrm[...] = (tok * scale * gain_ref[...]).astype(BF16)
    N[y_lo, y_hi, x, zrow, :] = nrm[:, half]
    C[y_lo, y_hi, x, zrow, :] = og_ref[:, half]
    pl.semaphore_wait(barrier, len(peers))

    def along_y(a, src, dst):
        row = {}
        for dy in (1, 2, 3):
            there = ((y + dy) % 4) // 2
            cols = pl.ds(pl.multiple_of(there * HALF, HALF), HALF)
            row[dy] = copy(src.at[:, cols], dst.at[y_lo, y_hi, x, zrow, :],
                           y_s.at[a, dy - 1], y_r.at[a, dy - 1], dev(dy=dy))
        return row

    y_copies = [along_y(0, nrm, N), along_y(1, og_ref, C)]

    def y_start(a, k):
        @pl.when(y_lo == k)
        def _():
            for dy in (1, 3, 2):
                y_copies[a][dy].start()

    def y_wait(a, k):
        @pl.when(y_lo == k)
        def _():
            y_copies[a][2].wait_recv()

        @pl.when(y_lo != k)
        def _():
            y_copies[a][1].wait_recv()
            y_copies[a][3].wait_recv()

    y_start(0, 0)
    GS[...] = jnp.zeros_like(GS)
    GQ[...] = jnp.zeros_like(GQ)

    def zr(i):
        return pl.ds(pl.multiple_of(((z + i) % 4) * ROWS, ROWS), ROWS)

    def ag_first(ref, k, p, off, yh):
        if p == 0:
            return ref.at[k, yh, (x + off) % 4, zrow, PART[0]]
        return ref.at[k, yh, x, zr(off), PART[1]]

    def ag_second(ref, k, p, off, yh):
        if p == 0:
            return ref.at[k, yh, :, zr(off), PART[0]]
        return ref.at[k, yh, (x + off) % 4, :, PART[1]]

    def ag_dev(p, phase, step):
        return dev(dx=step) if p == phase else dev(dz=step)

    units = [(N, 0), (C, 0), (N, 1), (C, 1)]

    def ag_block(u, phase, yh, off=0):
        ref, k = units[u]
        for p in (0, 1):
            for d, step in enumerate((1, -1)):
                block = ag_first(ref, k, p, off, yh)
                recv = ag_f.at[u, phase, p, d] if yh == d else ag_r.at[u, phase, 0]
                begin(block, block, ag_s.at[u, phase], recv, ag_dev(p, phase, step))

    def ag_early(a):
        for k in (0, 1):
            for yh in (0, 1):

                @pl.when(jnp.logical_and(y_lo == k, y_hi == yh))
                def _():
                    ag_block(a + 2 * k, 0, yh)
                    if k == 0:
                        ag_block(a, 1, yh)

    def ag_start(u):
        k = units[u][1]
        for yh in (0, 1):

            @pl.when(jnp.logical_or(y_lo != k, y_hi != yh))
            def _():
                ag_block(u, 0, yh)
                if k == 0:
                    ag_block(u, 1, yh)

    def ag_piece(u, offs):
        for off in offs:
            for yh in (0, 1):
                ag_block(u, 1, yh, off)

    def ag_own(u):
        ref, k = units[u]
        for first in (0, 1):
            for p in (0, 1):
                for d, step in enumerate((1, -1)):
                    block = ag_second(ref, k, p, 0, d if first == 0 else 1 - d)
                    recv = ag_f.at[u, 1, p, d] if first == 0 else ag_r.at[u, 1, 0]
                    begin(block, block, ag_s.at[u, 1], recv, ag_dev(p, 1, step))

    def ag_fwd(u, phase):
        ref, k = units[u]
        where = (ag_first, ag_second)[phase]
        for p in (0, 1):
            for d, step in enumerate((1, -1)):
                take(ag_f.at[u, phase, p, d], blocks((1, 4)[phase]))
                block = where(ref, k, p, -step, d)
                begin(block, block, ag_s.at[u, phase], ag_r.at[u, phase, 1], ag_dev(p, phase, step))

    def ag_wait(u, phase, i):
        take(ag_r.at[u, phase, i - 1], blocks((4, 16)[phase]))

    def ag_end(u, phase):
        if phase == 0:
            ag_wait(u, phase, 1)
        ag_wait(u, phase, 2)

    def ag_sent():
        for u in range(4):
            for phase in (0, 1):
                take(ag_s.at[u, phase], blocks((12, 48)[phase]))

    partner = dev(dy=2)

    def rows_of(ref, k, yh):
        return ref[k, yh].reshape(PATCHES, HALF)

    def partial_in(k):
        other = 1 - y_hi

        @pl.loop(0, W_IN // TILE, unroll=3)
        def _(j):
            cols = pl.ds(pl.multiple_of(j * TILE, TILE), TILE)
            XS[k, :, cols] = dot(rows_of(N, k, other), win[:, cols], ((1,), (0,))).astype(BF16)

        cp = send(XS.at[k, :, pl.ds(0, W_IN)], XR.at[k, :, pl.ds(0, W_IN)], e_s.at[k, 0], e_r.at[k, 0], partner)

        @pl.loop(0, W_IN // TILE, unroll=3)
        def _(j):
            cols = pl.ds(pl.multiple_of(j * TILE, TILE), TILE)
            H[k, :, cols] = dot(rows_of(N, k, y_hi), win[:, cols], ((1,), (0,)))

        return cp

    def partial_out(k):
        other = 1 - y_hi

        @pl.loop(0, W_OUT // TILE, unroll=2)
        def _(j):
            rows = pl.ds(pl.multiple_of(j * TILE, TILE), TILE)
            cols = pl.ds(pl.multiple_of(W_IN + j * TILE, TILE), TILE)
            XS[k, :, cols] = dot(rows_of(C, k, other), wout[rows, :], ((1,), (1,))).astype(BF16)

        cp = send(XS.at[k, :, pl.ds(W_IN, W_OUT)], XR.at[k, :, pl.ds(W_IN, W_OUT)],
                  e_s.at[k, 1], e_r.at[k, 1], partner)

        @pl.loop(0, W_OUT // TILE, unroll=2)
        def _(j):
            rows = pl.ds(pl.multiple_of(j * TILE, TILE), TILE)
            cols = pl.ds(pl.multiple_of(W_IN + j * TILE, TILE), TILE)
            H[k, :, cols] = dot(rows_of(C, k, y_hi), wout[rows, :], ((1,), (1,)))

        return cp

    def summed(k, start, width, rows=slice(None)):
        cols = pl.ds(start, width)
        return H[k, rows, cols] + XR[k, rows, cols].astype(F32)

    def head_norm(h, g):
        factor = lax.rsqrt(jnp.mean(h * h, axis=1, keepdims=True) + EPS)
        return factor, (h * factor * g).astype(BF16)

    def head_norm_back(h, factor, g, dy):
        hf = h * factor
        dyg = dy * g
        dh = factor * (dyg - hf * jnp.mean(hf * dyg, axis=1, keepdims=True))
        return dh, jnp.sum(dy * hf, axis=0, keepdims=True)

    def middle(k):
        hq, hk = summed(k, 0, HEAD), summed(k, HEAD, HEAD)
        v = summed(k, 2 * HEAD, HEAD).astype(BF16)
        da = summed(k, W_IN, HEAD).astype(BF16)
        qg, kg = qg_ref[...], kg_ref[...]
        fq, qn = head_norm(hq, qg)
        fk, kn = head_norm(hk, kg)
        w = jnp.exp(dot(qn, kn, ((1,), (1,))) * HEAD**-0.5)
        probs = w / jnp.sum(w, axis=1, keepdims=True)
        probs_b = probs.astype(BF16)
        ACT[k, y_hi, :, 0:HEAD] = dot(probs_b, v, ((1,), (0,))).astype(BF16)
        dpr = dot(da, v, ((1,), (1,))).astype(BF16).astype(F32)
        HG[k, y_hi, :, 2 * HEAD : 3 * HEAD] = dot(probs_b, da, ((0,), (0,))).astype(BF16)
        ds = probs * (dpr - jnp.sum(probs * dpr, axis=1, keepdims=True))
        ds = (ds * HEAD**-0.5).astype(BF16)
        dqn = dot(ds, kn, ((1,), (0,))).astype(BF16).astype(F32)
        dkn = dot(ds, qn, ((0,), (0,))).astype(BF16).astype(F32)
        dhq, dqg = head_norm_back(hq, fq, qg, dqn)
        dhk, dkg = head_norm_back(hk, fk, kg, dkn)
        HG[k, y_hi, :, 0:HEAD] = dhq.astype(BF16)
        HG[k, y_hi, :, HEAD : 2 * HEAD] = dhk.astype(BF16)
        GQ[0:1, :] += dqg
        GQ[1:2, :] += dkg

        @pl.loop(0, 4)
        def _(i):
            rows = pl.ds(pl.multiple_of(i * 64, 64), 64)
            u = summed(k, 3 * HEAD, UP, rows)
            dact = summed(k, W_IN + HEAD, UP, rows).astype(BF16).astype(F32)
            t = jnp.tanh(GELU_A * (u + GELU_B * (u * u * u)))
            ACT[k, y_hi, rows, HEAD:] = (0.5 * u * (1.0 + t)).astype(BF16)
            slope = 0.5 * (1.0 + t) + 0.5 * u * (1.0 - t * t) * (GELU_A * (1.0 + 3.0 * GELU_B * (u * u)))
            HG[k, y_hi, rows, 3 * HEAD :] = (dact * slope).astype(BF16)

        return send(HG.at[k, y_hi], HG.at[k, y_hi], e_s.at[k, 2], e_r.at[k, 2], partner)

    def swap_act(k):
        return send(ACT.at[k, y_hi], ACT.at[k, y_hi], e_s.at[k, 3], e_r.at[k, 3], partner)

    def normed_grad(k, yh):
        @pl.loop(0, HALF // WIDE, unroll=2)
        def _(j):
            cols = pl.ds(pl.multiple_of(j * WIDE, WIDE), WIDE)
            ng = dot(HG[k, yh], win[cols, :], ((1,), (1,)))
            G[k, yh, :, :, cols] = ng.astype(BF16).reshape(4, 64, WIDE)
            term = ng * N[k, yh, :, :, cols].reshape(PATCHES, WIDE).astype(F32)
            GS[:, cols] += jnp.sum(term.reshape(PATCHES // 8, 8, WIDE), axis=0)

    def rs_bufs(k, phase, p):
        if phase == 1:
            return (FB1, FB2)[p].at[k], (MB1, MB2)[p].at[k]
        return FS.at[p, k], MS.at[p, k]

    def rs_cut(phase, p, view, s):
        cols = pl.ds(s * SUB, SUB)
        return view.at[:, :, cols] if phase == 1 and p == 0 else view.at[:, cols]

    def rs_steps(k, phase, yh):
        where = (ag_first, ag_second)[phase]
        for p in (0, 1):
            fr, mr = rs_bufs(k, phase, p)
            for s, step in enumerate((1, -1)):
                block = lambda off: rs_cut(phase, p, where(G, k, p, off, yh), s)
                far = rs_cut(phase, p, fr.at[yh], s)
                near = [rs_cut(phase, p, mr.at[i, yh], s) for i in (0, 1)]
                yield p, step, block, far, near

    def rs_far(k, phase, yh):
        for p, step, block, far, _ in rs_steps(k, phase, yh):
            begin(block(2), far, rs_s.at[k, phase, yh], rs_f.at[k, phase, yh], ag_dev(p, phase, step))

    def rs_near(k, phase, yh):
        for p, step, block, _, near in rs_steps(k, phase, yh):
            begin(block(-step), near[1], rs_s.at[k, phase, yh], rs_r.at[k, phase, yh], ag_dev(p, phase, -step))

    def rs_start(k, phase, yh):
        rs_far(k, phase, yh)
        rs_near(k, phase, yh)

    def rs_mid(k, phase, yh):
        take(rs_f.at[k, phase, yh], blocks((2, 8)[phase]))
        for p, step, block, far, near in rs_steps(k, phase, yh):
            mine = block(step)
            mine[...] = (mine[...].astype(F32) + far[...].astype(F32)).astype(BF16)
            begin(mine, near[0], rs_s.at[k, phase, yh], rs_r.at[k, phase, yh], ag_dev(p, phase, step))

    def rs_end(k, phase, yh):
        take(rs_r.at[k, phase, yh], blocks((4, 16)[phase]))
        where = (ag_first, ag_second)[phase]
        for p in (0, 1):
            _, mr = rs_bufs(k, phase, p)
            block = where(G, k, p, 0, yh)
            total = block[...].astype(F32) + mr[0, yh].astype(F32) + mr[1, yh].astype(F32)
            block[...] = total.astype(BF16)

    def rs_sent():
        for k in (0, 1):
            for phase in (0, 1):
                for yh in (0, 1):
                    take(rs_s.at[k, phase, yh], blocks((6, 24)[phase]))

    def feature_tile(t, whose):
        return pl.ds(pl.multiple_of(whose * QUART + t * TILE, TILE), TILE)

    def grad_in(t, whose, k):
        left = N[k, :, :, :, feature_tile(t, whose)].reshape(2 * PATCHES, TILE)
        return dot(left, HG[k].reshape(2 * PATCHES, W_IN), ((0,), (0,)))

    def grad_out(t, whose, yh):
        right = C[:, yh, :, :, feature_tile(t, whose)].reshape(2 * PATCHES, TILE)
        return dot(ACT[:, yh].reshape(2 * PATCHES, W_OUT), right, ((0,), (0,)))

    def swap(kind, t):
        src, dst = ((SD, RD), (SO, RO))[kind]
        return copy(src.at[t], dst.at[t], d_s.at[kind], d_r.at[kind, t], dev(dc=1))

    tiles = QUART // TILE

    def tile_rows(t):
        return pl.ds(pl.multiple_of(t * TILE, TILE), TILE)

    def keep_in(t, total):
        for j in range(3):
            dqkv_ref[j, tile_rows(t), :] = total[:, j * HEAD : (j + 1) * HEAD].astype(BF16)
        dup_ref[tile_rows(t), :] = total[:, 3 * HEAD :].astype(BF16)

    def in_first(lo, hi):
        @pl.loop(lo, hi, unroll=3)
        def _(t):
            SD[t] = grad_in(t, 1 - core, 0).astype(BF16)
            keep_in(t, grad_in(t, core, 0))

    def keep_out(t, total):
        dproj_ref[:, tile_rows(t)] = total[:HEAD].astype(BF16)
        ddown_ref[:, tile_rows(t)] = total[HEAD:].astype(BF16)

    def out_first():
        @pl.loop(0, tiles, unroll=3)
        def _(t):
            SO[t] = grad_out(t, 1 - core, y_hi).astype(BF16)
            keep_out(t, grad_out(t, core, y_hi))

    def in_away(lo, hi):
        @pl.loop(lo, hi)
        def _(t):
            SD[t] = (SD[t].astype(F32) + grad_in(t, 1 - core, 1)).astype(BF16)
            swap(0, t).start()

    def out_away(lo, hi):
        @pl.loop(lo, hi)
        def _(t):
            SO[t] = (SO[t].astype(F32) + grad_out(t, 1 - core, 1 - y_hi)).astype(BF16)
            swap(1, t).start()

    def in_here(lo, hi):
        @pl.loop(lo, hi)
        def _(t):
            second = grad_in(t, core, 1)
            swap(0, t).wait_recv()
            kept = [dqkv_ref[j, tile_rows(t), :] for j in range(3)] + [dup_ref[tile_rows(t), :]]
            first = jnp.concatenate(kept, axis=1).astype(F32)
            keep_in(t, first + second + RD[t].astype(F32))

    def out_here(lo, hi):
        @pl.loop(lo, hi)
        def _(t):
            second = grad_out(t, core, 1 - y_hi)
            swap(1, t).wait_recv()
            kept = [dproj_ref[:, tile_rows(t)], ddown_ref[:, tile_rows(t)]]
            first = jnp.concatenate(kept, axis=0).astype(F32)
            keep_out(t, first + second + RO[t].astype(F32))

    def gain_send(stage, slots, me, tos):
        for to in tos:
            begin(slots.at[me], slots.at[me], g_s.at[stage], g_r.at[stage], to)

    gain_slots = [GC.at[0:1], GY.at[0:3], GX.at[0:3], GZ.at[0:3]]

    def gain_wait(stage):
        take(g_r.at[stage], gain_slots[stage])

    def gain_sent():
        for stage in range(4):
            take(g_s.at[stage], gain_slots[stage])

    def wait_all(cps):
        for cp in cps:
            cp.wait_recv()

    def owner_copy(dy):
        yy = (y + dy) % 4
        return copy(
            G.at[yy % 2, yy // 2, x, zrow, :], YR.at[y], z_s.at[dy - 1], z_r.at[dy - 1], dev(dy=dy)
        )

    def to_owner(k):
        @pl.when(y_lo == k)
        def _():
            owner_copy(2).start()

        @pl.when(y_lo != k)
        def _():
            owner_copy(1).start()
            owner_copy(3).start()

    results = ((dqkv_ref, dqkv_hbm), (dup_ref, dup_hbm), (dproj_ref, dproj_hbm), (ddown_ref, ddown_hbm))
    stores = [pltpu.make_async_copy(src, dst, osem.at[i]) for i, (src, dst) in enumerate(results)]

    own, other = y_hi, 1 - y_hi
    ag_early(0)
    ag_early(1)
    y_wait(0, 0)
    y_start(1, 0)
    ag_start(0)
    y_wait(1, 0)
    ag_start(1)
    y_start(0, 1)
    y_start(1, 1)
    ag_fwd(0, 0)
    ag_wait(0, 0, 1)
    ag_piece(0, (1, -1))
    ag_wait(0, 0, 2)
    ag_piece(0, (2,))
    ag_fwd(1, 0)
    y_wait(0, 1)
    ag_start(2)
    ag_fwd(0, 1)
    ag_end(1, 0)
    ag_piece(1, (1, -1, 2))
    ag_fwd(2, 0)
    for cp in loads:
        cp.wait()
    y_wait(1, 1)
    ag_start(3)
    ag_wait(0, 1, 1)
    ag_end(0, 1)
    e_in0 = partial_in(0)
    ag_fwd(1, 1)
    ag_end(2, 0)
    ag_own(2)
    ag_fwd(3, 0)
    ag_wait(1, 1, 1)
    ag_end(1, 1)
    e_out0 = partial_out(0)
    ag_fwd(2, 1)
    ag_end(3, 0)
    ag_own(3)
    ag_wait(2, 1, 1)
    wait_all((e_in0, e_out0))
    back0 = middle(0)
    normed_grad(0, own)
    ag_end(2, 1)
    e_in1 = partial_in(1)
    ag_fwd(3, 1)
    back0.wait_recv()
    normed_grad(0, other)
    ag_wait(3, 1, 1)
    in_first(0, 3)
    ag_end(3, 1)
    rs_far(0, 1, own)
    rs_far(0, 1, other)
    e_out1 = partial_out(1)
    rs_near(0, 1, own)
    rs_near(0, 1, other)
    in_first(3, 6)
    rs_mid(0, 1, own)
    wait_all((e_in1, e_out1))
    back1 = middle(1)
    rs_mid(0, 1, other)
    normed_grad(1, own)
    rs_start(1, 1, own)
    rs_end(0, 1, own)
    rs_start(0, 0, own)
    rs_end(0, 1, other)
    rs_start(0, 0, other)
    out_first()
    back1.wait_recv()
    normed_grad(1, other)
    rs_start(1, 1, other)
    acts = [swap_act(0), swap_act(1)]
    rs_mid(0, 0, own)
    rs_mid(0, 0, other)
    rs_mid(1, 1, own)
    gsum = jnp.sum(GS[...], axis=0, keepdims=True)
    for j in range(HALF // HEAD):
        GC[core, j : j + 1, :] = gsum[:, j * HEAD : (j + 1) * HEAD]
    GC[core, 24:32, :] = GQ[...]
    gain_send(0, GC, core, [dev(dc=1)])
    in_away(0, 6)
    gain_wait(0)
    GY[y] = GC[0] + GC[1]
    gain_send(1, GY, y, [dev(dy=d) for d in (1, 2, 3)])
    rs_mid(1, 1, other)
    rs_end(0, 0, own)
    rs_end(0, 0, other)
    to_owner(0)
    rs_end(1, 1, own)
    rs_start(1, 0, own)
    in_here(0, 3)
    rs_end(1, 1, other)
    rs_start(1, 0, other)
    in_here(3, 6)
    for cp in stores[:2]:
        cp.start()
    gain_wait(1)
    GX[x, 0] = GY[0] + GY[1]
    GX[x, 1] = GY[2] + GY[3]
    gain_send(2, GX, x, [dev(dx=d) for d in (1, 2, 3)])
    rs_mid(1, 0, own)
    rs_mid(1, 0, other)
    wait_all(acts)
    out_away(0, 6)
    rs_end(1, 0, own)
    rs_end(1, 0, other)
    to_owner(1)
    YR[y] = G[y_lo, y_hi, x, zrow, :]
    gain_wait(2)
    GZ[z] = ((GX[0] + GX[1]) + GX[2]) + GX[3]
    gain_send(3, GZ, z, [dev(dz=d) for d in (1, 2, 3)])
    out_here(0, 6)
    for cp in stores[2:]:
        cp.start()
    ag_sent()
    rs_sent()
    gain_wait(3)
    gains = ((GZ[0] + GZ[1]) + GZ[2]) + GZ[3]
    for h in (0, 1):
        rows = slice(h * 24, (h + 1) * 24)
        gsum_ref[rows, :] = gains[h, 0:24, :] / gain_rows_ref[rows, :]
    qk_ref[...] = gains[0, 24:26, :] + gains[1, 24:26, :]
    for dy in (1, 2, 3):
        owner_copy(dy).wait_recv()
    inner = jnp.zeros((ROWS, 1), F32)
    for h in (0, 1):
        cols = slice(h * HALF, (h + 1) * HALF)
        c = (YR[2 * h].astype(F32) + YR[2 * h + 1].astype(F32)) * gain_ref[:, cols]
        inner += jnp.sum(c * tok_ref[:, cols].astype(F32), axis=1, keepdims=True)
    inner = inner / D
    for h in (0, 1):
        cols = slice(h * HALF, (h + 1) * HALF)
        c = (YR[2 * h].astype(F32) + YR[2 * h + 1].astype(F32)) * gain_ref[:, cols]
        own = tok_ref[:, cols].astype(F32)
        grad = og_ref[:, cols].astype(F32) + scale * c - own * (scale * scale * scale * inner)
        tg_ref[:, cols] = grad.astype(BF16)
    gain_sent()
    drain(len(pending))
    for cp in stores:
        cp.wait()
    for row in y_copies:
        for dy in (1, 2, 3):
            row[dy].wait_send()
    for dy in (1, 2, 3):
        owner_copy(dy).wait_send()
    take(d_s.at[0], SD)
    take(d_s.at[1], SO)


def per_device(tokens, norm_gain, qkv_weight, up_weight, proj_weight, down_weight, query_gain, key_gain, out_grad):
    vm, hbm = pl.BlockSpec(memory_space=pltpu.VMEM), pl.BlockSpec(memory_space=pl.ANY)
    tiles = QUART // TILE
    quarter = HALF // 2
    dma = pltpu.SemaphoreType.DMA
    scratch = [
        pltpu.VMEM((ROWS, D), BF16),
        pltpu.VMEM((2, 2, 4, 64, HALF), BF16),
        pltpu.VMEM((2, 2, 4, 64, HALF), BF16),
        pltpu.VMEM((2, 2, 4, 64, HALF), BF16),
        pltpu.VMEM((HALF, W_IN), BF16),
        pltpu.VMEM((W_OUT, HALF), BF16),
        pltpu.VMEM((2, PATCHES, W_IN + W_OUT), BF16),
        pltpu.VMEM((2, PATCHES, W_IN + W_OUT), BF16),
        pltpu.VMEM((2, PATCHES, W_IN + W_OUT), F32),
        pltpu.VMEM((2, 2, PATCHES, W_IN), BF16),
        pltpu.VMEM((2, 2, PATCHES, W_OUT), BF16),
        pltpu.VMEM((2, 2, 4, ROWS, quarter), BF16),
        pltpu.VMEM((2, 2, 2, 4, ROWS, quarter), BF16),
        pltpu.VMEM((2, 2, 64, quarter), BF16),
        pltpu.VMEM((2, 2, 2, 64, quarter), BF16),
        pltpu.VMEM((2, 2, 2, ROWS, quarter), BF16),
        pltpu.VMEM((2, 2, 2, 2, ROWS, quarter), BF16),
        pltpu.VMEM((4, ROWS, HALF), BF16),
        pltpu.VMEM((tiles, TILE, W_IN), BF16),
        pltpu.VMEM((tiles, TILE, W_IN), BF16),
        pltpu.VMEM((tiles, W_OUT, TILE), BF16),
        pltpu.VMEM((tiles, W_OUT, TILE), BF16),
        pltpu.VMEM((8, HALF), F32),
        pltpu.VMEM((8, HEAD), F32),
        pltpu.VMEM((2, 32, HEAD), F32),
        pltpu.VMEM((4, 32, HEAD), F32),
        pltpu.VMEM((4, 2, 32, HEAD), F32),
        pltpu.VMEM((4, 2, 32, HEAD), F32),
        pltpu.VMEM((3, QUART, HEAD), BF16),
        pltpu.VMEM((QUART, UP), BF16),
        pltpu.VMEM((HEAD, QUART), BF16),
        pltpu.VMEM((UP, QUART), BF16),
        dma((4,)),
        dma((6,)),
        dma((2, 3)),
        dma((2, 3)),
        dma((4, 2)),
        dma((4, 2, 2, 2)),
        dma((4, 2, 2)),
        dma((2, 4)),
        dma((2, 4)),
        dma((2, 2, 2)),
        dma((2, 2, 2)),
        dma((2, 2, 2)),
        dma((3,)),
        dma((3,)),
        dma((2,)),
        dma((2, tiles)),
        dma((4,)),
        dma((4,)),
    ]
    token_grad, gain_grad, qk_grad, dqkv, dup, dproj, ddown = pl.pallas_call(
        kernel,
        name="block",
        out_shape=(
            jax.ShapeDtypeStruct((ROWS, D), BF16),
            jax.ShapeDtypeStruct((D // HEAD, HEAD), F32),
            jax.ShapeDtypeStruct((2, HEAD), F32),
            jax.ShapeDtypeStruct((3, QUART, HEAD), BF16),
            jax.ShapeDtypeStruct((QUART, UP), BF16),
            jax.ShapeDtypeStruct((HEAD, QUART), BF16),
            jax.ShapeDtypeStruct((UP, QUART), BF16),
        ),
        in_specs=[vm] * 6 + [hbm] * 4,
        out_specs=(vm,) * 3 + (hbm,) * 4,
        scratch_shapes=scratch,
        compiler_params=pltpu.CompilerParams(
            collective_id=0, has_side_effects=True, vmem_limit_bytes=60 * 1024 * 1024
        ),
        cost_estimate=pl.CostEstimate(flops=21 * 10**9, bytes_accessed=20 * 10**6, transcendentals=0),
    )(
        tokens, out_grad, norm_gain.reshape(1, D), norm_gain.reshape(D // HEAD, HEAD),
        query_gain.reshape(1, HEAD), key_gain.reshape(1, HEAD),
        jnp.transpose(qkv_weight, (1, 0, 2)), up_weight, proj_weight, down_weight,
    )
    return finish(token_grad, gain_grad, qk_grad, dqkv, dup, dproj, ddown)


def widen(tg_ref, gain_ref, qk_ref, dqkv_ref, dup_ref, dproj_ref, ddown_ref, *outs):
    tg_out, gain_out, qk_out, dqkv_out, dup_out, dproj_out, ddown_out = outs

    @pl.when(pl.program_id(0) == 0)
    def _():
        tg_out[...] = tg_ref[...]
        gain_out[...] = gain_ref[...]
        qk_out[...] = qk_ref[...]

    for src, dst in ((dqkv_ref, dqkv_out), (dup_ref, dup_out), (dproj_ref, dproj_out), (ddown_ref, ddown_out)):
        dst[...] = src[...].astype(F32)


def finish(*arrays):
    steps = 2
    block = QUART // steps
    whole = [pl.BlockSpec(a.shape, lambda i: (0, 0)) for a in arrays[:3]]
    specs = whole + [
        pl.BlockSpec((3, block, HEAD), lambda i: (0, i, 0)),
        pl.BlockSpec((block, UP), lambda i: (i, 0)),
        pl.BlockSpec((HEAD, block), lambda i: (0, i)),
        pl.BlockSpec((UP, block), lambda i: (0, i)),
    ]
    shapes = [jax.ShapeDtypeStruct(a.shape, a.dtype) for a in arrays[:3]]
    shapes += [jax.ShapeDtypeStruct(a.shape, F32) for a in arrays[3:]]
    token_grad, gain_grad, qk_grad, dqkv, dup, dproj, ddown = pl.pallas_call(
        widen, name="widen", grid=(steps,), in_specs=specs, out_specs=specs, out_shape=shapes
    )(*arrays)
    return token_grad, gain_grad.reshape(D), qk_grad, jnp.transpose(dqkv, (1, 0, 2)), dup, dproj, ddown


def solution(mesh):
    rows = P(("dp", "mp"), None)
    placed = (rows, P(), P(None, None, "mp"), P(None, "mp"), P("mp", None), P("mp", None), P(), P(), rows)
    outs = (rows, P(), P(), P("dp", None, "mp"), P("dp", "mp"), P("mp", "dp"), P("mp", "dp"))
    return jax.shard_map(per_device, mesh=mesh, in_specs=placed, out_specs=outs, check_vma=False)
```

```python
import jax
import jax.numpy as jnp
from jax import lax
from jax.experimental import pallas as pl
from jax.experimental.pallas import tpu as pltpu
from jax.sharding import PartitionSpec as P

F32, BF16 = jnp.float32, jnp.bfloat16
MESH = pl.DeviceIdType.MESH

D = 6144
HALF = D // 2
QUART = D // 4
PATCHES = 256
HEAD = 128
UP = 384
W_IN = 3 * HEAD + UP
W_OUT = HEAD + UP
ROWS = 16
TILE = 256
WIDE = 512
PART = (slice(0, HALF // 2), slice(HALF // 2, HALF))
SUB = HALF // 4
EPS = 1e-06
GELU_A, GELU_B = 0.7978845608028654, 0.044715


def dot(left, right, dims):
    return lax.dot_general(left, right, (dims, ((), ())), preferred_element_type=F32)


def kernel(
    tok_in, og_in, gain_in, gain_rows_in, qg_in, kg_in, wqkv_ref, wup_ref, wproj_ref, wdown_ref,
    tg_ref, gsum_ref, qk_ref, dqkv_hbm, dup_hbm, dproj_hbm, ddown_hbm,
    tok_ref, og_ref, gain_ref, gain_rows_ref, qg_ref, kg_ref, isem, nrm, N, C, G, win, wout, XS, XR, H, HG, ACT, FB1, MB1, FB2, MB2, FS, MS, YR,
    SD, RD, SO, RO, GS, GQ, GC, GY, GX, GZ,
    dqkv_ref, dup_ref, dproj_ref, ddown_ref, osem, wsem, y_s, y_r, ag_s, ag_f, ag_r, e_s, e_r, rs_s, rs_f, rs_r, z_s, z_r, d_s, d_r, g_s, g_r,
):
    dp, mp = lax.axis_index("dp"), lax.axis_index("mp")
    y_hi, core = dp // 2, dp % 2
    y_lo, x, z = mp // 16, (mp // 4) % 4, mp % 4
    y = y_hi * 2 + y_lo

    def dev(dx=0, dy=0, dz=0, dc=0):
        xx, yy, zz, cc = (x + dx) % 4, (y + dy) % 4, (z + dz) % 4, (core + dc) % 2
        return ((yy // 2) * 2 + cc, (yy % 2) * 16 + xx * 4 + zz)

    def copy(src, dst, send, recv, to):
        return pltpu.make_async_remote_copy(
            src_ref=src, dst_ref=dst, send_sem=send, recv_sem=recv, device_id=to, device_id_type=MESH
        )

    pending = []

    def begin(*args):
        cp = copy(*args)
        cp.start()
        return cp

    def take(sem, view):
        pltpu.make_async_copy(view, view, sem).wait()

    def blocks(count):
        rows, cols = {1: (16, 1), 2: (32, 1), 6: (32, 1), 24: (64, 2)}.get(count, (64, 1))
        groups = count * ROWS // (rows * cols)
        if count == 48:
            return N.at[0, :, 0:3]
        return N.at[0, 0, 0:groups, 0:rows, 0 : cols * (HALF // 2)]

    def drain(upto):
        for cp in pending[:upto]:
            cp.wait_send()
        del pending[:upto]

    def send(*args):
        cp = copy(*args)
        cp.start()
        pending.append(cp)
        return cp

    barrier = pltpu.get_barrier_semaphore()
    peers = [dev(dy=d) for d in (1, 2, 3)] + [dev(dx=d) for d in (1, 2, 3)]
    peers += [dev(dz=d) for d in (1, 2, 3)] + [dev(dc=1)]
    for peer in peers:
        pl.semaphore_signal(barrier, inc=1, device_id=peer, device_id_type=MESH)

    zrow = pl.ds(pl.multiple_of(z * ROWS, ROWS), ROWS)

    inputs = ((tok_in, tok_ref), (gain_in, gain_ref), (og_in, og_ref), (gain_rows_in, gain_rows_ref), (qg_in, qg_ref),
              (kg_in, kg_ref))
    reads = [pltpu.make_async_copy(src, dst, isem.at[i]) for i, (src, dst) in enumerate(inputs)]
    for cp in reads:
        cp.start()

    half = pl.ds(pl.multiple_of(y_hi * HALF, HALF), HALF)
    loads = [
        pltpu.make_async_copy(wqkv_ref.at[j, half], win.at[:, pl.ds(j * HEAD, HEAD)], wsem.at[j])
        for j in range(3)
    ]
    loads.append(pltpu.make_async_copy(wup_ref.at[half], win.at[:, pl.ds(3 * HEAD, UP)], wsem.at[3]))
    loads.append(pltpu.make_async_copy(wproj_ref.at[:, half], wout.at[pl.ds(0, HEAD)], wsem.at[4]))
    loads.append(pltpu.make_async_copy(wdown_ref.at[:, half], wout.at[pl.ds(HEAD, UP)], wsem.at[5]))
    for cp in loads:
        cp.start()


    for cp in reads:
        cp.wait()
    tok = tok_ref[...].astype(F32)
    scale = lax.rsqrt(jnp.mean(tok * tok, axis=1, keepdims=True) + EPS)
    nrm[...] = (tok * scale * gain_ref[...]).astype(BF16)
    N[y_lo, y_hi, x, zrow, :] = nrm[:, half]
    C[y_lo, y_hi, x, zrow, :] = og_ref[:, half]
    pl.semaphore_wait(barrier, len(peers))

    def along_y(a, src, dst):
        row = {}
        for dy in (1, 2, 3):
            there = ((y + dy) % 4) // 2
            cols = pl.ds(pl.multiple_of(there * HALF, HALF), HALF)
            row[dy] = copy(src.at[:, cols], dst.at[y_lo, y_hi, x, zrow, :],
                           y_s.at[a, dy - 1], y_r.at[a, dy - 1], dev(dy=dy))
        return row

    y_copies = [along_y(0, nrm, N), along_y(1, og_ref, C)]

    def y_start(a, k):
        @pl.when(y_lo == k)
        def _():
            for dy in (1, 3, 2):
                y_copies[a][dy].start()

    def y_wait(a, k):
        @pl.when(y_lo == k)
        def _():
            y_copies[a][2].wait_recv()

        @pl.when(y_lo != k)
        def _():
            y_copies[a][1].wait_recv()
            y_copies[a][3].wait_recv()

    y_start(0, 0)
    GS[...] = jnp.zeros_like(GS)
    GQ[...] = jnp.zeros_like(GQ)

    def zr(i):
        return pl.ds(pl.multiple_of(((z + i) % 4) * ROWS, ROWS), ROWS)

    def ag_first(ref, k, p, off, yh):
        if p == 0:
            return ref.at[k, yh, (x + off) % 4, zrow, PART[0]]
        return ref.at[k, yh, x, zr(off), PART[1]]

    def ag_second(ref, k, p, off, yh):
        if p == 0:
            return ref.at[k, yh, :, zr(off), PART[0]]
        return ref.at[k, yh, (x + off) % 4, :, PART[1]]

    def ag_dev(p, phase, step):
        return dev(dx=step) if p == phase else dev(dz=step)

    units = [(N, 0), (C, 0), (N, 1), (C, 1)]

    def ag_block(u, phase, yh, off=0):
        ref, k = units[u]
        for p in (0, 1):
            for d, step in enumerate((1, -1)):
                block = ag_first(ref, k, p, off, yh)
                recv = ag_f.at[u, phase, p, d] if yh == d else ag_r.at[u, phase, 0]
                begin(block, block, ag_s.at[u, phase], recv, ag_dev(p, phase, step))

    def ag_early(a):
        for k in (0, 1):
            for yh in (0, 1):

                @pl.when(jnp.logical_and(y_lo == k, y_hi == yh))
                def _():
                    ag_block(a + 2 * k, 0, yh)
                    if k == 0:
                        ag_block(a, 1, yh)

    def ag_start(u):
        k = units[u][1]
        for yh in (0, 1):

            @pl.when(jnp.logical_or(y_lo != k, y_hi != yh))
            def _():
                ag_block(u, 0, yh)
                if k == 0:
                    ag_block(u, 1, yh)

    def ag_piece(u, offs):
        for off in offs:
            for yh in (0, 1):
                ag_block(u, 1, yh, off)

    def ag_own(u):
        ref, k = units[u]
        for first in (0, 1):
            for p in (0, 1):
                for d, step in enumerate((1, -1)):
                    block = ag_second(ref, k, p, 0, d if first == 0 else 1 - d)
                    recv = ag_f.at[u, 1, p, d] if first == 0 else ag_r.at[u, 1, 0]
                    begin(block, block, ag_s.at[u, 1], recv, ag_dev(p, 1, step))

    def ag_fwd(u, phase):
        ref, k = units[u]
        where = (ag_first, ag_second)[phase]
        for p in (0, 1):
            for d, step in enumerate((1, -1)):
                take(ag_f.at[u, phase, p, d], blocks((1, 4)[phase]))
                block = where(ref, k, p, -step, d)
                begin(block, block, ag_s.at[u, phase], ag_r.at[u, phase, 1], ag_dev(p, phase, step))

    def ag_wait(u, phase, i):
        take(ag_r.at[u, phase, i - 1], blocks((4, 16)[phase]))

    def ag_end(u, phase):
        if phase == 0:
            ag_wait(u, phase, 1)
        ag_wait(u, phase, 2)

    def ag_sent():
        for u in range(4):
            for phase in (0, 1):
                take(ag_s.at[u, phase], blocks((12, 48)[phase]))

    partner = dev(dy=2)

    def rows_of(ref, k, yh):
        return ref[k, yh].reshape(PATCHES, HALF)

    def partial_in(k):
        other = 1 - y_hi

        @pl.loop(0, W_IN // TILE, unroll=3)
        def _(j):
            cols = pl.ds(pl.multiple_of(j * TILE, TILE), TILE)
            XS[k, :, cols] = dot(rows_of(N, k, other), win[:, cols], ((1,), (0,))).astype(BF16)

        cp = send(XS.at[k, :, pl.ds(0, W_IN)], XR.at[k, :, pl.ds(0, W_IN)], e_s.at[k, 0], e_r.at[k, 0], partner)

        @pl.loop(0, W_IN // TILE, unroll=3)
        def _(j):
            cols = pl.ds(pl.multiple_of(j * TILE, TILE), TILE)
            H[k, :, cols] = dot(rows_of(N, k, y_hi), win[:, cols], ((1,), (0,)))

        return cp

    def partial_out(k):
        other = 1 - y_hi

        @pl.loop(0, W_OUT // TILE, unroll=2)
        def _(j):
            rows = pl.ds(pl.multiple_of(j * TILE, TILE), TILE)
            cols = pl.ds(pl.multiple_of(W_IN + j * TILE, TILE), TILE)
            XS[k, :, cols] = dot(rows_of(C, k, other), wout[rows, :], ((1,), (1,))).astype(BF16)

        cp = send(XS.at[k, :, pl.ds(W_IN, W_OUT)], XR.at[k, :, pl.ds(W_IN, W_OUT)],
                  e_s.at[k, 1], e_r.at[k, 1], partner)

        @pl.loop(0, W_OUT // TILE, unroll=2)
        def _(j):
            rows = pl.ds(pl.multiple_of(j * TILE, TILE), TILE)
            cols = pl.ds(pl.multiple_of(W_IN + j * TILE, TILE), TILE)
            H[k, :, cols] = dot(rows_of(C, k, y_hi), wout[rows, :], ((1,), (1,)))

        return cp

    def summed(k, start, width, rows=slice(None)):
        cols = pl.ds(start, width)
        return H[k, rows, cols] + XR[k, rows, cols].astype(F32)

    def head_norm(h, g):
        factor = lax.rsqrt(jnp.mean(h * h, axis=1, keepdims=True) + EPS)
        return factor, (h * factor * g).astype(BF16)

    def head_norm_back(h, factor, g, dy):
        hf = h * factor
        dyg = dy * g
        dh = factor * (dyg - hf * jnp.mean(hf * dyg, axis=1, keepdims=True))
        return dh, jnp.sum(dy * hf, axis=0, keepdims=True)

    def middle(k):
        hq, hk = summed(k, 0, HEAD), summed(k, HEAD, HEAD)
        v = summed(k, 2 * HEAD, HEAD).astype(BF16)
        da = summed(k, W_IN, HEAD).astype(BF16)
        qg, kg = qg_ref[...], kg_ref[...]
        fq, qn = head_norm(hq, qg)
        fk, kn = head_norm(hk, kg)
        w = jnp.exp(dot(qn, kn, ((1,), (1,))) * HEAD**-0.5)
        probs = w / jnp.sum(w, axis=1, keepdims=True)
        probs_b = probs.astype(BF16)
        ACT[k, y_hi, :, 0:HEAD] = dot(probs_b, v, ((1,), (0,))).astype(BF16)
        dpr = dot(da, v, ((1,), (1,))).astype(BF16).astype(F32)
        HG[k, y_hi, :, 2 * HEAD : 3 * HEAD] = dot(probs_b, da, ((0,), (0,))).astype(BF16)
        ds = probs * (dpr - jnp.sum(probs * dpr, axis=1, keepdims=True))
        ds = (ds * HEAD**-0.5).astype(BF16)
        dqn = dot(ds, kn, ((1,), (0,))).astype(BF16).astype(F32)
        dkn = dot(ds, qn, ((0,), (0,))).astype(BF16).astype(F32)
        dhq, dqg = head_norm_back(hq, fq, qg, dqn)
        dhk, dkg = head_norm_back(hk, fk, kg, dkn)
        HG[k, y_hi, :, 0:HEAD] = dhq.astype(BF16)
        HG[k, y_hi, :, HEAD : 2 * HEAD] = dhk.astype(BF16)
        GQ[0:1, :] += dqg
        GQ[1:2, :] += dkg

        @pl.loop(0, 4)
        def _(i):
            rows = pl.ds(pl.multiple_of(i * 64, 64), 64)
            u = summed(k, 3 * HEAD, UP, rows)
            dact = summed(k, W_IN + HEAD, UP, rows).astype(BF16).astype(F32)
            t = jnp.tanh(GELU_A * (u + GELU_B * (u * u * u)))
            ACT[k, y_hi, rows, HEAD:] = (0.5 * u * (1.0 + t)).astype(BF16)
            slope = 0.5 * (1.0 + t) + 0.5 * u * (1.0 - t * t) * (GELU_A * (1.0 + 3.0 * GELU_B * (u * u)))
            HG[k, y_hi, rows, 3 * HEAD :] = (dact * slope).astype(BF16)

        return send(HG.at[k, y_hi], HG.at[k, y_hi], e_s.at[k, 2], e_r.at[k, 2], partner)

    def swap_act(k):
        return send(ACT.at[k, y_hi], ACT.at[k, y_hi], e_s.at[k, 3], e_r.at[k, 3], partner)

    def normed_grad(k, yh):
        @pl.loop(0, HALF // WIDE, unroll=2)
        def _(j):
            cols = pl.ds(pl.multiple_of(j * WIDE, WIDE), WIDE)
            ng = dot(HG[k, yh], win[cols, :], ((1,), (1,)))
            G[k, yh, :, :, cols] = ng.astype(BF16).reshape(4, 64, WIDE)
            term = ng * N[k, yh, :, :, cols].reshape(PATCHES, WIDE).astype(F32)
            GS[:, cols] += jnp.sum(term.reshape(PATCHES // 8, 8, WIDE), axis=0)

    def rs_bufs(k, phase, p):
        if phase == 1:
            return (FB1, FB2)[p].at[k], (MB1, MB2)[p].at[k]
        return FS.at[p, k], MS.at[p, k]

    def rs_cut(phase, p, view, s):
        cols = pl.ds(s * SUB, SUB)
        return view.at[:, :, cols] if phase == 1 and p == 0 else view.at[:, cols]

    def rs_steps(k, phase, yh):
        where = (ag_first, ag_second)[phase]
        for p in (0, 1):
            fr, mr = rs_bufs(k, phase, p)
            for s, step in enumerate((1, -1)):
                block = lambda off: rs_cut(phase, p, where(G, k, p, off, yh), s)
                far = rs_cut(phase, p, fr.at[yh], s)
                near = [rs_cut(phase, p, mr.at[i, yh], s) for i in (0, 1)]
                yield p, step, block, far, near

    def rs_far(k, phase, yh):
        for p, step, block, far, _ in rs_steps(k, phase, yh):
            begin(block(2), far, rs_s.at[k, phase, yh], rs_f.at[k, phase, yh], ag_dev(p, phase, step))

    def rs_near(k, phase, yh):
        for p, step, block, _, near in rs_steps(k, phase, yh):
            begin(block(-step), near[1], rs_s.at[k, phase, yh], rs_r.at[k, phase, yh], ag_dev(p, phase, -step))

    def rs_start(k, phase, yh):
        rs_far(k, phase, yh)
        rs_near(k, phase, yh)

    def rs_mid(k, phase, yh):
        take(rs_f.at[k, phase, yh], blocks((2, 8)[phase]))
        for p, step, block, far, near in rs_steps(k, phase, yh):
            mine = block(step)
            mine[...] = (mine[...].astype(F32) + far[...].astype(F32)).astype(BF16)
            begin(mine, near[0], rs_s.at[k, phase, yh], rs_r.at[k, phase, yh], ag_dev(p, phase, step))

    def rs_end(k, phase, yh):
        take(rs_r.at[k, phase, yh], blocks((4, 16)[phase]))
        where = (ag_first, ag_second)[phase]
        for p in (0, 1):
            _, mr = rs_bufs(k, phase, p)
            block = where(G, k, p, 0, yh)
            total = block[...].astype(F32) + mr[0, yh].astype(F32) + mr[1, yh].astype(F32)
            block[...] = total.astype(BF16)

    def rs_sent():
        for k in (0, 1):
            for phase in (0, 1):
                for yh in (0, 1):
                    take(rs_s.at[k, phase, yh], blocks((6, 24)[phase]))

    def feature_tile(t, whose):
        return pl.ds(pl.multiple_of(whose * QUART + t * TILE, TILE), TILE)

    def grad_in(t, whose, k):
        left = N[k, :, :, :, feature_tile(t, whose)].reshape(2 * PATCHES, TILE)
        return dot(left, HG[k].reshape(2 * PATCHES, W_IN), ((0,), (0,)))

    def grad_out(t, whose, yh):
        right = C[:, yh, :, :, feature_tile(t, whose)].reshape(2 * PATCHES, TILE)
        return dot(ACT[:, yh].reshape(2 * PATCHES, W_OUT), right, ((0,), (0,)))

    def swap(kind, t):
        src, dst = ((SD, RD), (SO, RO))[kind]
        return copy(src.at[t], dst.at[t], d_s.at[kind], d_r.at[kind, t], dev(dc=1))

    tiles = QUART // TILE

    def tile_rows(t):
        return pl.ds(pl.multiple_of(t * TILE, TILE), TILE)

    def keep_in(t, total):
        for j in range(3):
            dqkv_ref[j, tile_rows(t), :] = total[:, j * HEAD : (j + 1) * HEAD].astype(BF16)
        dup_ref[tile_rows(t), :] = total[:, 3 * HEAD :].astype(BF16)

    def in_first(lo, hi):
        @pl.loop(lo, hi, unroll=3)
        def _(t):
            SD[t] = grad_in(t, 1 - core, 0).astype(BF16)
            keep_in(t, grad_in(t, core, 0))

    def keep_out(t, total):
        dproj_ref[:, tile_rows(t)] = total[:HEAD].astype(BF16)
        ddown_ref[:, tile_rows(t)] = total[HEAD:].astype(BF16)

    def out_first():
        @pl.loop(0, tiles, unroll=3)
        def _(t):
            SO[t] = grad_out(t, 1 - core, y_hi).astype(BF16)
            keep_out(t, grad_out(t, core, y_hi))

    def in_away(lo, hi):
        @pl.loop(lo, hi)
        def _(t):
            SD[t] = (SD[t].astype(F32) + grad_in(t, 1 - core, 1)).astype(BF16)
            swap(0, t).start()

    def out_away(lo, hi):
        @pl.loop(lo, hi)
        def _(t):
            SO[t] = (SO[t].astype(F32) + grad_out(t, 1 - core, 1 - y_hi)).astype(BF16)
            swap(1, t).start()

    def in_here(lo, hi):
        @pl.loop(lo, hi)
        def _(t):
            second = grad_in(t, core, 1)
            swap(0, t).wait_recv()
            kept = [dqkv_ref[j, tile_rows(t), :] for j in range(3)] + [dup_ref[tile_rows(t), :]]
            first = jnp.concatenate(kept, axis=1).astype(F32)
            keep_in(t, first + second + RD[t].astype(F32))

    def out_here(lo, hi):
        @pl.loop(lo, hi)
        def _(t):
            second = grad_out(t, core, 1 - y_hi)
            swap(1, t).wait_recv()
            kept = [dproj_ref[:, tile_rows(t)], ddown_ref[:, tile_rows(t)]]
            first = jnp.concatenate(kept, axis=0).astype(F32)
            keep_out(t, first + second + RO[t].astype(F32))

    def gain_send(stage, slots, me, tos):
        for to in tos:
            begin(slots.at[me], slots.at[me], g_s.at[stage], g_r.at[stage], to)

    gain_slots = [GC.at[0:1], GY.at[0:3], GX.at[0:3], GZ.at[0:3]]

    def gain_wait(stage):
        take(g_r.at[stage], gain_slots[stage])

    def gain_sent():
        for stage in range(4):
            take(g_s.at[stage], gain_slots[stage])

    def wait_all(cps):
        for cp in cps:
            cp.wait_recv()

    def owner_copy(dy):
        yy = (y + dy) % 4
        return copy(
            G.at[yy % 2, yy // 2, x, zrow, :], YR.at[y], z_s.at[dy - 1], z_r.at[dy - 1], dev(dy=dy)
        )

    def to_owner(k):
        @pl.when(y_lo == k)
        def _():
            owner_copy(2).start()

        @pl.when(y_lo != k)
        def _():
            owner_copy(1).start()
            owner_copy(3).start()

    results = ((dqkv_ref, dqkv_hbm), (dup_ref, dup_hbm), (dproj_ref, dproj_hbm), (ddown_ref, ddown_hbm))
    stores = [pltpu.make_async_copy(src, dst, osem.at[i]) for i, (src, dst) in enumerate(results)]

    own, other = y_hi, 1 - y_hi
    ag_early(0)
    ag_early(1)
    y_wait(0, 0)
    y_start(1, 0)
    ag_start(0)
    y_wait(1, 0)
    ag_start(1)
    y_start(0, 1)
    y_start(1, 1)
    ag_fwd(0, 0)
    ag_wait(0, 0, 1)
    ag_piece(0, (1, -1))
    ag_wait(0, 0, 2)
    ag_piece(0, (2,))
    ag_fwd(1, 0)
    y_wait(0, 1)
    ag_start(2)
    ag_fwd(0, 1)
    ag_end(1, 0)
    ag_piece(1, (1, -1, 2))
    ag_fwd(2, 0)
    for cp in loads:
        cp.wait()
    y_wait(1, 1)
    ag_start(3)
    ag_wait(0, 1, 1)
    ag_end(0, 1)
    e_in0 = partial_in(0)
    ag_fwd(1, 1)
    ag_end(2, 0)
    ag_own(2)
    ag_fwd(3, 0)
    ag_wait(1, 1, 1)
    ag_end(1, 1)
    e_out0 = partial_out(0)
    ag_fwd(2, 1)
    ag_end(3, 0)
    ag_own(3)
    ag_wait(2, 1, 1)
    wait_all((e_in0, e_out0))
    back0 = middle(0)
    normed_grad(0, own)
    ag_end(2, 1)
    e_in1 = partial_in(1)
    ag_fwd(3, 1)
    back0.wait_recv()
    normed_grad(0, other)
    ag_wait(3, 1, 1)
    in_first(0, 3)
    ag_end(3, 1)
    rs_far(0, 1, own)
    rs_far(0, 1, other)
    e_out1 = partial_out(1)
    rs_near(0, 1, own)
    rs_near(0, 1, other)
    in_first(3, 6)
    rs_mid(0, 1, own)
    wait_all((e_in1, e_out1))
    back1 = middle(1)
    rs_mid(0, 1, other)
    normed_grad(1, own)
    rs_start(1, 1, own)
    rs_end(0, 1, own)
    rs_start(0, 0, own)
    rs_end(0, 1, other)
    rs_start(0, 0, other)
    out_first()
    back1.wait_recv()
    normed_grad(1, other)
    rs_start(1, 1, other)
    acts = [swap_act(0), swap_act(1)]
    rs_mid(0, 0, own)
    rs_mid(0, 0, other)
    rs_mid(1, 1, own)
    gsum = jnp.sum(GS[...], axis=0, keepdims=True)
    for j in range(HALF // HEAD):
        GC[core, j : j + 1, :] = gsum[:, j * HEAD : (j + 1) * HEAD]
    GC[core, 24:32, :] = GQ[...]
    gain_send(0, GC, core, [dev(dc=1)])
    in_away(0, 6)
    gain_wait(0)
    GY[y] = GC[0] + GC[1]
    gain_send(1, GY, y, [dev(dy=d) for d in (1, 2, 3)])
    rs_mid(1, 1, other)
    rs_end(0, 0, own)
    rs_end(0, 0, other)
    to_owner(0)
    rs_end(1, 1, own)
    rs_start(1, 0, own)
    in_here(0, 3)
    rs_end(1, 1, other)
    rs_start(1, 0, other)
    in_here(3, 6)
    for cp in stores[:2]:
        cp.start()
    gain_wait(1)
    GX[x, 0] = GY[0] + GY[1]
    GX[x, 1] = GY[2] + GY[3]
    gain_send(2, GX, x, [dev(dx=d) for d in (1, 2, 3)])
    rs_mid(1, 0, own)
    rs_mid(1, 0, other)
    wait_all(acts)
    out_away(0, 6)
    rs_end(1, 0, own)
    rs_end(1, 0, other)
    to_owner(1)
    YR[y] = G[y_lo, y_hi, x, zrow, :]
    gain_wait(2)
    GZ[z] = ((GX[0] + GX[1]) + GX[2]) + GX[3]
    gain_send(3, GZ, z, [dev(dz=d) for d in (1, 2, 3)])
    out_here(0, 6)
    for cp in stores[2:]:
        cp.start()
    ag_sent()
    rs_sent()
    gain_wait(3)
    gains = ((GZ[0] + GZ[1]) + GZ[2]) + GZ[3]
    for h in (0, 1):
        rows = slice(h * 24, (h + 1) * 24)
        gsum_ref[rows, :] = gains[h, 0:24, :] / gain_rows_ref[rows, :]
    qk_ref[...] = gains[0, 24:26, :] + gains[1, 24:26, :]
    for dy in (1, 2, 3):
        owner_copy(dy).wait_recv()
    inner = jnp.zeros((ROWS, 1), F32)
    for h in (0, 1):
        cols = slice(h * HALF, (h + 1) * HALF)
        c = (YR[2 * h].astype(F32) + YR[2 * h + 1].astype(F32)) * gain_ref[:, cols]
        inner += jnp.sum(c * tok_ref[:, cols].astype(F32), axis=1, keepdims=True)
    inner = inner / D
    for h in (0, 1):
        cols = slice(h * HALF, (h + 1) * HALF)
        c = (YR[2 * h].astype(F32) + YR[2 * h + 1].astype(F32)) * gain_ref[:, cols]
        own = tok_ref[:, cols].astype(F32)
        grad = og_ref[:, cols].astype(F32) + scale * c - own * (scale * scale * scale * inner)
        tg_ref[:, cols] = grad.astype(BF16)
    gain_sent()
    drain(len(pending))
    for cp in stores:
        cp.wait()
    for row in y_copies:
        for dy in (1, 2, 3):
            row[dy].wait_send()
    for dy in (1, 2, 3):
        owner_copy(dy).wait_send()
    take(d_s.at[0], SD)
    take(d_s.at[1], SO)


def per_device(tokens, norm_gain, qkv_weight, up_weight, proj_weight, down_weight, query_gain, key_gain, out_grad):
    vm, hbm = pl.BlockSpec(memory_space=pltpu.VMEM), pl.BlockSpec(memory_space=pl.ANY)
    tiles = QUART // TILE
    quarter = HALF // 2
    dma = pltpu.SemaphoreType.DMA
    scratch = [
        pltpu.VMEM((ROWS, D), BF16),
        pltpu.VMEM((ROWS, D), BF16),
        pltpu.VMEM((1, D), F32),
        pltpu.VMEM((D // HEAD, HEAD), F32),
        pltpu.VMEM((1, HEAD), F32),
        pltpu.VMEM((1, HEAD), F32),
        dma((6,)),
        pltpu.VMEM((ROWS, D), BF16),
        pltpu.VMEM((2, 2, 4, 64, HALF), BF16),
        pltpu.VMEM((2, 2, 4, 64, HALF), BF16),
        pltpu.VMEM((2, 2, 4, 64, HALF), BF16),
        pltpu.VMEM((HALF, W_IN), BF16),
        pltpu.VMEM((W_OUT, HALF), BF16),
        pltpu.VMEM((2, PATCHES, W_IN + W_OUT), BF16),
        pltpu.VMEM((2, PATCHES, W_IN + W_OUT), BF16),
        pltpu.VMEM((2, PATCHES, W_IN + W_OUT), F32),
        pltpu.VMEM((2, 2, PATCHES, W_IN), BF16),
        pltpu.VMEM((2, 2, PATCHES, W_OUT), BF16),
        pltpu.VMEM((2, 2, 4, ROWS, quarter), BF16),
        pltpu.VMEM((2, 2, 2, 4, ROWS, quarter), BF16),
        pltpu.VMEM((2, 2, 64, quarter), BF16),
        pltpu.VMEM((2, 2, 2, 64, quarter), BF16),
        pltpu.VMEM((2, 2, 2, ROWS, quarter), BF16),
        pltpu.VMEM((2, 2, 2, 2, ROWS, quarter), BF16),
        pltpu.VMEM((4, ROWS, HALF), BF16),
        pltpu.VMEM((tiles, TILE, W_IN), BF16),
        pltpu.VMEM((tiles, TILE, W_IN), BF16),
        pltpu.VMEM((tiles, W_OUT, TILE), BF16),
        pltpu.VMEM((tiles, W_OUT, TILE), BF16),
        pltpu.VMEM((8, HALF), F32),
        pltpu.VMEM((8, HEAD), F32),
        pltpu.VMEM((2, 32, HEAD), F32),
        pltpu.VMEM((4, 32, HEAD), F32),
        pltpu.VMEM((4, 2, 32, HEAD), F32),
        pltpu.VMEM((4, 2, 32, HEAD), F32),
        pltpu.VMEM((3, QUART, HEAD), BF16),
        pltpu.VMEM((QUART, UP), BF16),
        pltpu.VMEM((HEAD, QUART), BF16),
        pltpu.VMEM((UP, QUART), BF16),
        dma((4,)),
        dma((6,)),
        dma((2, 3)),
        dma((2, 3)),
        dma((4, 2)),
        dma((4, 2, 2, 2)),
        dma((4, 2, 2)),
        dma((2, 4)),
        dma((2, 4)),
        dma((2, 2, 2)),
        dma((2, 2, 2)),
        dma((2, 2, 2)),
        dma((3,)),
        dma((3,)),
        dma((2,)),
        dma((2, tiles)),
        dma((4,)),
        dma((4,)),
    ]
    token_grad, gain_grad, qk_grad, dqkv, dup, dproj, ddown = pl.pallas_call(
        kernel,
        name="block",
        out_shape=(
            jax.ShapeDtypeStruct((ROWS, D), BF16),
            jax.ShapeDtypeStruct((D // HEAD, HEAD), F32),
            jax.ShapeDtypeStruct((2, HEAD), F32),
            jax.ShapeDtypeStruct((3, QUART, HEAD), BF16),
            jax.ShapeDtypeStruct((QUART, UP), BF16),
            jax.ShapeDtypeStruct((HEAD, QUART), BF16),
            jax.ShapeDtypeStruct((UP, QUART), BF16),
        ),
        in_specs=[hbm] * 10,
        out_specs=(vm,) * 3 + (hbm,) * 4,
        scratch_shapes=scratch,
        compiler_params=pltpu.CompilerParams(
            collective_id=0, has_side_effects=True, vmem_limit_bytes=60 * 1024 * 1024
        ),
        cost_estimate=pl.CostEstimate(flops=21 * 10**9, bytes_accessed=20 * 10**6, transcendentals=0),
    )(
        tokens, out_grad, norm_gain.reshape(1, D), norm_gain.reshape(D // HEAD, HEAD),
        query_gain.reshape(1, HEAD), key_gain.reshape(1, HEAD),
        jnp.transpose(qkv_weight, (1, 0, 2)), up_weight, proj_weight, down_weight,
    )
    return finish(token_grad, gain_grad, qk_grad, dqkv, dup, dproj, ddown)


def widen(tg_ref, gain_ref, qk_ref, dqkv_ref, dup_ref, dproj_ref, ddown_ref, *outs):
    tg_out, gain_out, qk_out, dqkv_out, dup_out, dproj_out, ddown_out = outs

    @pl.when(pl.program_id(0) == 0)
    def _():
        tg_out[...] = tg_ref[...]
        gain_out[...] = gain_ref[...]
        qk_out[...] = qk_ref[...]

    for src, dst in ((dqkv_ref, dqkv_out), (dup_ref, dup_out), (dproj_ref, dproj_out), (ddown_ref, ddown_out)):
        dst[...] = src[...].astype(F32)


def finish(*arrays):
    steps = 2
    block = QUART // steps
    whole = [pl.BlockSpec(a.shape, lambda i: (0, 0)) for a in arrays[:3]]
    specs = whole + [
        pl.BlockSpec((3, block, HEAD), lambda i: (0, i, 0)),
        pl.BlockSpec((block, UP), lambda i: (i, 0)),
        pl.BlockSpec((HEAD, block), lambda i: (0, i)),
        pl.BlockSpec((UP, block), lambda i: (0, i)),
    ]
    shapes = [jax.ShapeDtypeStruct(a.shape, a.dtype) for a in arrays[:3]]
    shapes += [jax.ShapeDtypeStruct(a.shape, F32) for a in arrays[3:]]
    token_grad, gain_grad, qk_grad, dqkv, dup, dproj, ddown = pl.pallas_call(
        widen, name="widen", grid=(steps,), in_specs=specs, out_specs=specs, out_shape=shapes
    )(*arrays)
    return token_grad, gain_grad.reshape(D), qk_grad, jnp.transpose(dqkv, (1, 0, 2)), dup, dproj, ddown


def solution(mesh):
    rows = P(("dp", "mp"), None)
    placed = (rows, P(), P(None, None, "mp"), P(None, "mp"), P("mp", None), P("mp", None), P(), P(), rows)
    outs = (rows, P(), P(), P("dp", None, "mp"), P("dp", "mp"), P("mp", "dp"), P("mp", "dp"))
    return jax.shard_map(per_device, mesh=mesh, in_specs=placed, out_specs=outs, check_vma=False)
```
